512 devices in a mesh: leaf: 128 (over z, y, core), sub: 4 (over x).
Axes of the slice: x: 4, y: 8, z: 8, core: 2. Of those that a mesh axis runs over, the one named last changes fastest.
Arguments:
- light: bfloat16 [32, 1048576], P(None, ('leaf', 'sub')), may hold values from -6 to 6
- probes: bfloat16 [4, 1048576], P(None, ('leaf', 'sub')), may hold values from 0 to 1, as said below
- near_list: int32 [4096, 4], P(('leaf', 'sub')), may hold values from 0 to 4095, as said below
- far_list: int32 [4096, 32], P(('leaf', 'sub')), may hold values from 0 to 4095, as said below
- leaf_basis: bfloat16 [4096, 256, 64], P(('leaf', 'sub')), may hold values from -0.375 to 0.375
- leaf_transfer: bfloat16 [4096, 64, 64], P(('leaf', 'sub')), may hold values from -0.25 to 0.25
- far_coupling: bfloat16 [4096, 32, 64, 64], P(('leaf', 'sub')), may hold values from -0.125 to 0.125
- up_transfer: bfloat16 [3, 2, 64, 64], replicated, may hold values from -0.5 to 0.5
- upper_coupling: bfloat16 [4, 2, 64, 64], replicated, may hold values from -0.5 to 0.5
Outputs:
- irradiance: bfloat16 [32, 1048576], P(None, ('leaf', 'sub'))
The draws below stay inside these ranges and needn't reach their ends.
Inputs may be any that keep to these rules, and one draw needn't show every extreme that they name: `near_list`: each leaf's list names 4 distinct leaves other than itself, each within 4 leaf numbers of it. `far_list`: every entry names a leaf on a device with the same sub index as the leaf's own device and another leaf index. The entries of one device's leaves name leaves of any one other device at most 4 times, and exactly 4 times for some device. `probes`: rows 0 to 2 lie in the unit box, row 3 is positive.
All inputs are finite; a program needn't handle non-finite values.
Results may differ from the reference program's by a relative error of at most 0.0049.
The reference program's roundings to bfloat16 on the way count: a program that leaves them out, or rounds other values in their place, can miss the bound.
Values may be sent and summed in bfloat16 or wider, within the bound.
A program may use at most 128 MiB of HBM per device.

```python
import math
import jax
import jax.numpy as jnp
from jax import lax

LEAF = 256
RANK = 64
LIGHTS = 32
LEAVES_DEV = 8
HALO = 4
NNEAR = 4
NFAR = 32
UPLV = 3
NLEAF = 4096
PROBES = 1048576
CAP = 4
N_LEAF = 128
N_SUB = 4


def draw_probes(key, part):
    key = jax.random.fold_in(key, 11)
    first_key, second_key = jax.random.split(key)
    places = jax.random.uniform(first_key, (3, PROBES), jnp.float32)
    albedo = jnp.exp(jax.random.uniform(second_key, (1, PROBES), jnp.float32, math.log(0.25), 0.0))
    return jnp.concatenate([places, albedo], axis=0).astype(jnp.bfloat16)


def draw_near_list(key, part):
    key = jax.random.fold_in(key, 23)
    offsets = jnp.concatenate([-jnp.arange(1, HALO + 1), jnp.arange(1, HALO + 1)]).astype(jnp.int32)
    leaf_ids = jnp.arange(NLEAF, dtype=jnp.int32)
    ranking = jax.vmap(lambda leaf_key: jax.random.permutation(leaf_key, 2 * HALO))(jax.random.split(key, NLEAF))
    ranking = ranking.astype(jnp.int32)
    targets = leaf_ids[:, None] + offsets[None, :]
    valid = (targets >= 0) & (targets < NLEAF)
    scores = jnp.where(valid, ranking, ranking + 4 * HALO)
    chosen = jnp.argsort(scores, axis=1, stable=True)[:, :NNEAR]
    return jnp.take_along_axis(targets, chosen, axis=1).astype(jnp.int32)


def draw_far_list(key, part):
    key = jax.random.fold_in(key, 37)
    devices = N_LEAF * N_SUB
    entry_count = LEAVES_DEV * NFAR
    capacity = CAP

    def device_draw(device_key, device):
        first_key, second_key, third_key, fourth_key = jax.random.split(device_key, 4)
        own_row = device // N_SUB
        own_group = device % N_SUB
        forced = (own_row + 1 + jax.random.randint(first_key, (), 0, N_LEAF - 1)) % N_LEAF
        slots = jnp.arange(N_LEAF * capacity, dtype=jnp.int32)
        owner = slots // capacity
        priority = jax.random.permutation(second_key, N_LEAF * capacity).astype(jnp.int32)
        priority = jnp.where(owner == forced, slots % capacity - capacity, priority)
        priority = jnp.where(owner == own_row, priority + 2 * N_LEAF * capacity, priority)
        taken = jnp.argsort(priority, stable=True)[:entry_count]
        taken = jax.random.permutation(third_key, taken)
        peer_row = taken // capacity
        which_leaf = jax.random.randint(fourth_key, (entry_count,), 0, LEAVES_DEV)
        return ((peer_row * N_SUB + own_group) * LEAVES_DEV + which_leaf).astype(jnp.int32)
    drawn = jax.vmap(device_draw)(jax.random.split(key, devices), jnp.arange(devices, dtype=jnp.int32))
    return drawn.reshape(NLEAF, NFAR)


def shard_levels(key, extent, cuts, low, largest):
    gain = 1.0
    for position, parts in cuts:
        heights = jax.random.uniform(jax.random.fold_in(jax.random.fold_in(key, 6), position), (parts,), jnp.float32, low / len(cuts), largest / len(cuts))
        gain = gain * jnp.repeat(jnp.exp(heights), extent[position] // parts).reshape((-1,) + (1,) * (len(extent) - 1 - position))
    return gain


def gaussian(stream_key, shape, deviation, limit, pieces=(), kind=jnp.bfloat16):
    values = deviation * jax.random.normal(stream_key, shape, jnp.float32)
    if pieces:
        values = values * shard_levels(stream_key, shape, pieces, -0.22, 0.18)
    return jnp.clip(values, -limit, limit).astype(kind)


def setup_inputs(seed: int = 0) -> dict:
    keys = jax.random.split(jax.random.key(seed), 10)
    return {
        "light": gaussian(keys[0], (LIGHTS, PROBES), 1.0, 6.0, ((1, 512),)),
        "probes": draw_probes(jax.random.fold_in(keys[9], 71), 0),
        "near_list": draw_near_list(jax.random.fold_in(keys[9], 71), 0),
        "far_list": draw_far_list(jax.random.fold_in(keys[9], 71), 0),
        "leaf_basis": gaussian(keys[4], (NLEAF, LEAF, RANK), LEAF ** -0.5, 0.375, ((0, 512),)),
        "leaf_transfer": gaussian(keys[5], (NLEAF, RANK, RANK), (RANK * LEAVES_DEV) ** -0.5, 0.25, ((0, 512),)),
        "far_coupling": gaussian(keys[6], (NLEAF, NFAR, RANK, RANK), (RANK * NFAR) ** -0.5, 0.125, ((0, 512),)),
        "up_transfer": gaussian(keys[7], (UPLV, 2, RANK, RANK), (2 * RANK) ** -0.5, 0.5),
        "upper_coupling": gaussian(keys[8], (UPLV + 1, 2, RANK, RANK), (2 * RANK) ** -0.5, 0.5),
    }


soften = 0.0025
spacing = 0.25


def kernel_block(target_geo, source_geo, offset):
    delta_x = target_geo[0][:, None] - source_geo[0][None, :] + spacing * offset
    delta_y = target_geo[1][:, None] - source_geo[1][None, :]
    delta_z = target_geo[2][:, None] - source_geo[2][None, :]
    square = delta_x * delta_x + delta_y * delta_y + delta_z * delta_z
    return target_geo[3][:, None] * source_geo[3][None, :] * (soften / (soften + square))


def times_high(left_matrix, right_matrix):
    return jnp.einsum("crk,km->crm", left_matrix, right_matrix.astype(jnp.float32), precision=lax.Precision.HIGHEST)


def reference(light, probes, near_list, far_list, leaf_basis, leaf_transfer, far_coupling, up_transfer, upper_coupling):
    devices = N_LEAF * N_SUB
    geometry = probes.astype(jnp.float32).reshape(4, NLEAF, LEAF)
    blocks = light.reshape(LIGHTS, NLEAF, LEAF)
    coefficients = jnp.einsum("rtl,tlk->trk", blocks.astype(jnp.float32), leaf_basis.astype(jnp.float32)).astype(jnp.bfloat16)
    leaf_ids = jnp.arange(NLEAF, dtype=jnp.int32)
    partner = jnp.concatenate([leaf_ids[:, None], near_list.astype(jnp.int32)], axis=1)

    def near_leaf(target, sources):
        target_geo = lax.dynamic_index_in_dim(geometry, target, 1, keepdims=False)

        def one_block(source):
            source_geo = lax.dynamic_index_in_dim(geometry, source, 1, keepdims=False)
            values = lax.dynamic_index_in_dim(blocks, source, 1, keepdims=False)
            offset = (target - source).astype(jnp.float32)
            kernel_tile = kernel_block(target_geo, source_geo, offset).astype(jnp.bfloat16)
            return lax.dot_general(values, kernel_tile, (((1,), (1,)), ((), ())), preferred_element_type=jnp.float32)

        return jnp.sum(jax.vmap(one_block)(sources), axis=0)

    near_terms = lax.map(lambda leaf_pair: jax.vmap(near_leaf)(leaf_pair[0], leaf_pair[1]),
                         (leaf_ids.reshape(devices, LEAVES_DEV), partner.reshape(devices, LEAVES_DEV, NNEAR + 1)))

    def far_device(leaf_pair):
        picked = coefficients[leaf_pair[0]].astype(jnp.float32)
        return jnp.einsum("tcrk,tckm->trm", picked, leaf_pair[1].astype(jnp.float32))

    far_terms = lax.map(far_device, (far_list.reshape(devices, LEAVES_DEV, NFAR),
                                     far_coupling.reshape(devices, LEAVES_DEV, NFAR, RANK, RANK)))
    far_terms = far_terms.reshape(NLEAF, LIGHTS, RANK)
    leaf_terms = jnp.einsum("trk,tkm->trm", coefficients.astype(jnp.float32), leaf_transfer.astype(jnp.float32))
    upward = [jnp.sum(leaf_terms.reshape(devices, LEAVES_DEV, LIGHTS, RANK), axis=1)]
    for height in range(UPLV):
        sibling_pairs = upward[-1].reshape(-1, 2, LIGHTS, RANK)
        upward.append(times_high(sibling_pairs[:, 0], up_transfer[height, 0]) + times_high(sibling_pairs[:, 1], up_transfer[height, 1]))
    downward = None
    for height in range(UPLV, -1, -1):
        current = upward[height]
        zero_rim = jnp.zeros((2, LIGHTS, RANK), jnp.float32)
        padded = jnp.concatenate([zero_rim, current, zero_rim], axis=0)
        coupled = times_high(padded[:-4], upper_coupling[height, 0]) + times_high(padded[4:], upper_coupling[height, 1])
        if downward is not None:
            pushed = jnp.stack([times_high(downward, up_transfer[height, 0].T), times_high(downward, up_transfer[height, 1].T)], axis=1)
            coupled = coupled + pushed.reshape(-1, LIGHTS, RANK)
        downward = coupled
    pulled = jnp.einsum("trk,tmk->trm", jnp.repeat(downward, LEAVES_DEV, axis=0), leaf_transfer.astype(jnp.float32),
                        precision=lax.Precision.HIGHEST)
    leaf_far = (far_terms + pulled).astype(jnp.bfloat16)
    spread = jnp.einsum("trk,tlk->rtl", leaf_far.astype(jnp.float32), leaf_basis.astype(jnp.float32))
    combined = jnp.transpose(near_terms.reshape(NLEAF, LIGHTS, LEAF), (1, 0, 2)) + spread
    return combined.reshape(LIGHTS, PROBES).astype(jnp.bfloat16)
```

```python
import functools

import jax
import jax.numpy as jnp
from jax import lax
from jax.experimental import pallas as pl
from jax.experimental.pallas import tpu as pltpu
from jax.sharding import PartitionSpec as P

MESH = pl.DeviceIdType.MESH
F32, BF16 = jnp.float32, jnp.bfloat16
HIGH = lax.Precision.HIGHEST

HALO = 4
UPLV = 3
LEAF = 256
RANK = 64
LIGHTS = 32
LEAVES = 8
NNEAR = 4
NFAR = 32
soften = 0.0025
spacing = 0.25

RING = 8
LINE = RING * RING
PER_CHIP = 4
STEPS = RING * RING // 2
WHOLE = 16
HALVES = 24

NT = (((1,), (1,)), ((), ()))


def offset_of(j):
    return ((j + 1) // 2) * (1 - 2 * (j % 2))


def kernel(
    devices,
    light_hbm,
    probes_ref,
    near_list_ref,
    far_list_ref,
    basis_hbm,
    transfer_hbm,
    coupling_hbm,
    up_ref,
    upper_ref,
    out_ref,
    window,
    geo,
    columns,
    basis,
    transfer,
    coupling,
    pool,
    traded,
    near_terms,
    pulled,
    tile,
    upward,
    mine,
    partner,
    below,
    above,
    mask,
    load_sem,
    halo_send,
    halo_recv,
    trade_send,
    trade_recv,
    line_send,
    line_recv,
    right_send,
    right_recv,
    left_send,
    left_recv,
    sib_send,
    sib_recv,
    tree_send,
    tree_recv,
):
    leaf = lax.axis_index("leaf")
    sub = lax.axis_index("sub")
    me = leaf * 4 + sub
    core = leaf % 2
    y = (leaf // 2) % RING
    z = leaf // (2 * RING)
    first = y + core * (z - y)
    second = z + core * (y - z)

    def device(index):
        index = lax.rem(index + devices, devices)
        return (index // 4, lax.rem(index, 4))

    def chip(a, b):
        a = lax.rem(a + RING, RING)
        b = lax.rem(b + RING, RING)
        row = a + core * (b - a)
        layer = b + core * (a - b)
        return ((layer * RING + row) * 2 + core, sub)

    ahead, behind = chip(first + 1, second), chip(first - 1, second)
    right, left = chip(first, second + 1), chip(first, second - 1)
    sibling = (leaf + 1 - 2 * core, sub)

    def load(source, target, index):
        copy = pltpu.make_async_copy(source, target, load_sem.at[index])
        copy.start()
        return copy

    light_loads = [
        load(light_hbm.at[:, pl.ds(t * LEAF, LEAF)], window.at[HALO + t], 4 + t) for t in range(LEAVES)
    ]
    basis_load = load(basis_hbm, basis, 1)
    transfer_load = load(transfer_hbm, transfer, 2)
    coupling_load = load(coupling_hbm, coupling, 3)

    barrier = pltpu.get_barrier_semaphore()
    friends = [device(me + s * k) for k in (1, 2, 4, 8, 16) for s in (1, -1)]
    friends += [ahead, behind, right, left]
    for friend in friends:
        pl.semaphore_signal(barrier, inc=1, device_id=friend, device_id_type=MESH)

    geo[HALO : HALO + LEAVES] = jnp.zeros((LEAVES, 8, LEAF), F32)
    for t in range(LEAVES):
        geo[HALO + t, 0:4, :] = probes_ref[:, t * LEAF : (t + 1) * LEAF].astype(F32)
    lanes = lax.broadcasted_iota(jnp.int32, (LIGHTS, 2 * RANK), 1)
    mask[0] = jnp.where(lanes < RANK, 1.0, 0.0).astype(BF16)
    mask[1] = jnp.where(lanes < RANK, 0.0, 1.0).astype(BF16)

    pl.semaphore_wait(barrier, len(friends))

    def send(source, target, send_sem, recv_sem, to):
        return pltpu.make_async_remote_copy(
            src_ref=source,
            dst_ref=target,
            send_sem=send_sem,
            recv_sem=recv_sem,
            device_id=to,
            device_id_type=MESH,
        )

    pending = []

    def halo(ref, index):
        down = send(
            ref.at[pl.ds(HALO, HALO)],
            ref.at[pl.ds(HALO + LEAVES, HALO)],
            halo_send.at[index],
            halo_recv.at[index],
            device(me - 1),
        )
        up = send(
            ref.at[pl.ds(LEAVES, HALO)],
            ref.at[pl.ds(0, HALO)],
            halo_send.at[index + 1],
            halo_recv.at[index + 1],
            device(me + 1),
        )
        down.start()
        up.start()
        return [down, up]

    halos = halo(geo, 0)
    for light_load in light_loads:
        light_load.wait()
    basis_load.wait()

    chip_place = z * RING + y
    my_block = (core * LINE + chip_place) * PER_CHIP
    pairs = []
    for q in range(LEAVES // 2):
        parts = []
        for t in (2 * q, 2 * q + 1):
            parts.append(lax.dot_general(window[HALO + t], basis[t], NT, preferred_element_type=F32))
        pairs.append(jnp.concatenate(parts, axis=1).astype(BF16))
    for i in range(2):
        lower, higher = pairs[i], pairs[2 + i]
        pool[my_block + core * 2 + i] = jnp.where(core == 0, lower.astype(F32), higher.astype(F32)).astype(BF16)
        traded[i] = jnp.where(core == 0, higher.astype(F32), lower.astype(F32)).astype(BF16)
    other_block = ((1 - core) * LINE + chip_place) * PER_CHIP
    trade = send(
        traded,
        pool.at[pl.ds(other_block + core * 2, 2)],
        trade_send,
        trade_recv,
        sibling,
    )
    trade.start()
    pending.append(trade)
    halos += halo(window, 2)

    transfer_load.wait()
    stacked = jnp.concatenate(pairs, axis=1)
    level0 = jnp.dot(stacked, transfer[...], preferred_element_type=F32)

    def twice(value):
        return jnp.concatenate([value, value], axis=1)

    def matrix(value):
        return value.astype(F32)

    def climb(height, value):
        upward[height] = twice(value)
        stride = 2 ** (height + 1)
        moves = [
            send(
                upward.at[height],
                below.at[height],
                tree_send.at[3 * height],
                tree_recv.at[3 * height],
                device(me + stride),
            ),
            send(
                upward.at[height],
                above.at[height],
                tree_send.at[3 * height + 1],
                tree_recv.at[3 * height + 1],
                device(me - stride),
            ),
        ]
        if height < UPLV:
            parity = (me // 2**height) % 2
            mine[height] = twice(
                jnp.dot(value, matrix(up_ref[height, parity]), precision=HIGH, preferred_element_type=F32)
            )
            swap = send(
                mine.at[height],
                partner.at[height],
                tree_send.at[3 * height + 2],
                tree_recv.at[3 * height + 2],
                device(me + (1 - 2 * parity) * 2**height),
            )
            swap.start()
            moves.append(swap)
        moves[0].start()
        moves[1].start()
        return moves

    tree = [climb(0, level0)]

    half_base = core * LINE

    def block(a, b, count=PER_CHIP, skip=0):
        a = lax.rem(a + 2 * RING, RING)
        b = lax.rem(b + 2 * RING, RING)
        row, layer = a + core * (b - a), b + core * (a - b)
        return pool.at[pl.ds((half_base + layer * RING + row) * PER_CHIP + skip, count)]

    def line_copy(j, to):
        ref = block(first + offset_of(j), second)
        return send(ref, ref, line_send.at[j - 1], line_recv.at[j - 1], to)

    def ring_block(n, sign):
        return block(first + offset_of(n % RING), second - sign * (n // RING))

    def to_second(j):
        ref = block(first + offset_of(j), second)
        for sems, to in (
            ((right_send, right_recv), right),
            ((left_send, left_recv), left),
        ):
            send(ref, ref, sems[0].at[j], sems[1].at[j], to).start()
        send(ref, ref, sib_send.at[j], sib_recv.at[j], sibling).start()

    def line_send_of(j, hop, to):
        ref = block(first + offset_of(j), second)
        copy = send(ref, ref, line_send.at[hop - 1], line_recv.at[hop - 1], to)
        copy.start()
        pending_line.append(copy)

    pending_line = []
    trade.wait_recv()
    line_send_of(0, 1, ahead)
    line_send_of(0, 2, behind)
    to_second(0)

    def spread_columns(t):
        turned = jnp.transpose(geo[HALO + t])
        for k in range(4):
            value = turned[:, k : k + 1]
            if k == 3:
                value = value * soften
            columns[t, k] = jnp.broadcast_to(value, (LEAF, 128))

    for t in range(LEAVES):
        near_terms[t] = jnp.zeros((LIGHTS, LEAF), F32)

    def rejoin(height):
        tree[height][2].wait_recv()
        total = mine[height] + partner[height]
        tree.append(climb(height + 1, total[:, :RANK]))

    for j in range(1, RING):
        spread_columns(j - 1)
        if j == RING - 1:
            spread_columns(j)
        if j in (2, 4, 6):
            rejoin(j // 2 - 1)
        arrived = line_copy(j, ahead)
        arrived.wait_recv()
        hop = (j + 1) // 2
        if j % 2 == 1 and hop < RING // 2:
            line_send_of(j, j + 2, ahead)
        if j % 2 == 0 and hop < RING // 2 - 1:
            line_send_of(j, j + 2, behind)
        to_second(j)

    for move in halos:
        move.wait_recv()

    def near_pair(p):
        t, k = p // (NNEAR + 1), p % (NNEAR + 1)
        named = (near_list_ref[jnp.maximum(k - 1, 0), t] - LEAVES * me + HALO) & (LEAVES + 2 * HALO - 1)
        w = jnp.where(k == 0, t + HALO, named)
        shift = (t + HALO - w).astype(F32) * spacing
        rows = geo[w]
        row_x, row_y, row_z, row_a = (rows[0:1] - shift, rows[1:2], rows[2:3], rows[3:4])
        for i in range(0, LEAF, 32):
            sides = []
            for lane in (0, 128):
                cut = slice(lane, lane + 128)
                dx = columns[t, 0, i : i + 32] - row_x[:, cut]
                dy = columns[t, 1, i : i + 32] - row_y[:, cut]
                dz = columns[t, 2, i : i + 32] - row_z[:, cut]
                total = dx * dx + soften + dy * dy + dz * dz
                guess = pl.reciprocal(total, approx=True)
                guess = guess * (2.0 - total * guess)
                sides.append((columns[t, 3, i : i + 32] * row_a[:, cut] * guess).astype(BF16))
            tile[i : i + 32, :] = jnp.concatenate(sides, axis=1)
        near_terms[t] += lax.dot_general(window[w], tile[...], NT, preferred_element_type=F32)

    sides = (
        (1, right, right_send, right_recv, 0),
        (-1, left, left_send, left_recv, 2),
    )

    def half_block(n, sign, skip):
        return block(first + offset_of(n % RING), second - sign * (n // RING), 2, skip)

    def whole_step(n, carry):
        for side, (sign, to, send_sem, recv_sem, skip) in enumerate(sides):
            ref = block(first + offset_of(n % RING), second - sign * (n // RING + 1))
            send(ref, ref, send_sem.at[n], recv_sem.at[n], to).wait_recv()
            send(ref, ref, send_sem.at[n + RING], recv_sem.at[n + RING], to).start()
            index = RING + side * STEPS + n
            send(ref, ref, sib_send.at[index], sib_recv.at[index], sibling).start()
        near_pair(2 * n)
        near_pair(2 * n + 1)
        return carry

    def half_step(n, carry):
        for side, (sign, to, send_sem, recv_sem, skip) in enumerate(sides):
            a, b = first + offset_of(n % RING), second - sign * (n // RING + 1)
            ref, part = block(a, b), block(a, b, 2, skip)
            send(ref, ref, send_sem.at[n], recv_sem.at[n], to).wait_recv()
            send(part, part, send_sem.at[n + RING], recv_sem.at[n + RING], to).start()
            index = RING + side * STEPS + n
            send(ref, ref, sib_send.at[index], sib_recv.at[index], sibling).start()
        near_pair(WHOLE + n)
        return carry

    def last_step(n, carry):
        for side, (sign, to, send_sem, recv_sem, skip) in enumerate(sides):
            a, b = first + offset_of(n % RING), second - sign * (n // RING + 1)
            part = block(a, b, 2, skip)
            send(part, part, send_sem.at[n], recv_sem.at[n], to).wait_recv()
            index = RING + side * STEPS + n
            send(part, part, sib_send.at[index], sib_recv.at[index], sibling).start()
        return carry

    lax.fori_loop(0, WHOLE, whole_step, 0)
    lax.fori_loop(WHOLE, HALVES, half_step, 0)

    downward = None
    for height in range(UPLV, -1, -1):
        tree[height][0].wait_recv()
        tree[height][1].wait_recv()
        cluster = me // 2**height
        low = jnp.where(cluster >= 2, below[height][:, :RANK], 0.0)
        high = jnp.where(cluster + 2 < devices // 2**height, above[height][:, :RANK], 0.0)
        value = jnp.dot(low, matrix(upper_ref[height, 0]), precision=HIGH, preferred_element_type=F32)
        value += jnp.dot(high, matrix(upper_ref[height, 1]), precision=HIGH, preferred_element_type=F32)
        if downward is not None:
            parity = cluster % 2
            value += lax.dot_general(
                downward, matrix(up_ref[height, parity]), NT, precision=HIGH, preferred_element_type=F32
            )
        downward = value
    pulled[...] = lax.dot_general(
        downward, matrix(transfer[...]), NT, precision=HIGH, preferred_element_type=F32
    )

    lax.fori_loop(HALVES, STEPS, last_step, 0)

    coupling_load.wait()

    other_base = (1 - core) * LINE

    def other(a, b, count=PER_CHIP, skip=0):
        a = lax.rem(a + 2 * RING, RING)
        b = lax.rem(b + 2 * RING, RING)
        row, layer = b + core * (a - b), a + core * (b - a)
        return pool.at[pl.ds((other_base + layer * RING + row) * PER_CHIP + skip, count)]

    def wait_own(j, carry):
        ref = other(second + offset_of(j), first)
        send(ref, ref, sib_send.at[j], sib_recv.at[j], sibling).wait_recv()
        return carry

    def wait_whole(n, carry):
        for side, (sign, to, send_sem, recv_sem, skip) in enumerate(sides):
            ref = other(second + offset_of(n % RING), first - sign * (n // RING + 1))
            index = RING + side * STEPS + n
            send(ref, ref, sib_send.at[index], sib_recv.at[index], sibling).wait_recv()
        return carry

    def wait_part(n, carry):
        for side, (sign, to, send_sem, recv_sem, skip) in enumerate(sides):
            ref = other(second + offset_of(n % RING), first - sign * (n // RING + 1), 2, skip)
            index = RING + side * STEPS + n
            send(ref, ref, sib_send.at[index], sib_recv.at[index], sibling).wait_recv()
        return carry

    lax.fori_loop(0, RING, wait_own, 0)
    lax.fori_loop(0, HALVES, wait_whole, 0)
    lax.fori_loop(HALVES, STEPS, wait_part, 0)

    for t in range(LEAVES):
        picked, weights = [], []
        for c in range(NFAR):
            entry = far_list_ref[t, c]
            group, peer, pair = (entry >> 2) & 1, entry >> 5, (entry >> 1) & 1
            picked.append(pool[group * (LINE * PER_CHIP) + peer * 2 + pair] * mask[entry & 1])
            cut = coupling[t, c * RANK : (c + 1) * RANK, :]
            weights += [cut, cut]
        far = jnp.dot(
            jnp.concatenate(picked, axis=1),
            jnp.concatenate(weights, axis=0),
            preferred_element_type=F32,
        )
        leaf_far = (far + pulled[:, t * RANK : (t + 1) * RANK]).astype(BF16)
        back = jnp.dot(leaf_far, basis[t], preferred_element_type=F32)
        out_ref[:, t * LEAF : (t + 1) * LEAF] = (near_terms[t] + back).astype(BF16)

    trade.wait_send()
    for move in halos + pending_line + [m for moves in tree for m in moves]:
        move.wait_send()

    def sent_first(j, carry):
        ref = block(first + offset_of(j), second)
        for side, (sign, to, send_sem, recv_sem, skip) in enumerate(sides):
            send(ref, ref, send_sem.at[j], recv_sem.at[j], to).wait_send()
        send(ref, ref, sib_send.at[j], sib_recv.at[j], sibling).wait_send()
        return carry

    def sent_whole(n, carry):
        for side, (sign, to, send_sem, recv_sem, skip) in enumerate(sides):
            a, b = first + offset_of(n % RING), second - sign * (n // RING + 1)
            ref = block(a, b)
            send(ref, ref, send_sem.at[n + RING], recv_sem.at[n + RING], to).wait_send()
            index = RING + side * STEPS + n
            send(ref, ref, sib_send.at[index], sib_recv.at[index], sibling).wait_send()
        return carry

    def sent_half(n, carry):
        for side, (sign, to, send_sem, recv_sem, skip) in enumerate(sides):
            a, b = first + offset_of(n % RING), second - sign * (n // RING + 1)
            ref, part = block(a, b), block(a, b, 2, skip)
            send(part, part, send_sem.at[n + RING], recv_sem.at[n + RING], to).wait_send()
            index = RING + side * STEPS + n
            send(ref, ref, sib_send.at[index], sib_recv.at[index], sibling).wait_send()
        return carry

    def sent_part(n, carry):
        for side, (sign, to, send_sem, recv_sem, skip) in enumerate(sides):
            a, b = first + offset_of(n % RING), second - sign * (n // RING + 1)
            part = block(a, b, 2, skip)
            index = RING + side * STEPS + n
            send(part, part, sib_send.at[index], sib_recv.at[index], sibling).wait_send()
        return carry

    lax.fori_loop(0, RING, sent_first, 0)
    lax.fori_loop(0, WHOLE, sent_whole, 0)
    lax.fori_loop(WHOLE, HALVES, sent_half, 0)
    lax.fori_loop(HALVES, STEPS, sent_part, 0)


def solution(mesh):
    devices = mesh.shape["leaf"] * mesh.shape["sub"]

    def per_device(
        light,
        probes,
        near_list,
        far_list,
        leaf_basis,
        leaf_transfer,
        far_coupling,
        up_transfer,
        upper_coupling,
    ):
        any_space = pl.BlockSpec(memory_space=pl.ANY)
        vmem = pl.BlockSpec(memory_space=pltpu.VMEM)
        smem = pl.BlockSpec(memory_space=pltpu.SMEM)
        dma = pltpu.SemaphoreType.DMA
        slots = LEAVES + 2 * HALO
        return pl.pallas_call(
            functools.partial(kernel, devices),
            out_shape=jax.ShapeDtypeStruct((LIGHTS, LEAVES * LEAF), BF16),
            in_specs=[any_space, vmem, smem, smem, any_space, any_space, any_space, vmem, vmem],
            out_specs=vmem,
            scratch_shapes=[
                pltpu.VMEM((slots, LIGHTS, LEAF), BF16),
                pltpu.VMEM((slots, 8, LEAF), F32),
                pltpu.VMEM((LEAVES, 4, LEAF, 128), F32),
                pltpu.VMEM((LEAVES, RANK, LEAF), BF16),
                pltpu.VMEM((LEAVES * RANK, RANK), BF16),
                pltpu.VMEM((LEAVES, NFAR * RANK, RANK), BF16),
                pltpu.VMEM((2 * LINE * PER_CHIP, LIGHTS, 2 * RANK), BF16),
                pltpu.VMEM((2, LIGHTS, 2 * RANK), BF16),
                pltpu.VMEM((LEAVES, LIGHTS, LEAF), F32),
                pltpu.VMEM((LIGHTS, LEAVES * RANK), F32),
                pltpu.VMEM((LEAF, LEAF), BF16),
                pltpu.VMEM((UPLV + 1, LIGHTS, 2 * RANK), F32),
                pltpu.VMEM((UPLV, LIGHTS, 2 * RANK), F32),
                pltpu.VMEM((UPLV, LIGHTS, 2 * RANK), F32),
                pltpu.VMEM((UPLV + 1, LIGHTS, 2 * RANK), F32),
                pltpu.VMEM((UPLV + 1, LIGHTS, 2 * RANK), F32),
                pltpu.VMEM((2, LIGHTS, 2 * RANK), BF16),
                dma((4 + LEAVES,)),
                dma((4,)),
                dma((4,)),
                dma,
                dma,
                dma((RING - 1,)),
                dma((RING - 1,)),
                dma((STEPS,)),
                dma((STEPS,)),
                dma((STEPS,)),
                dma((STEPS,)),
                dma((RING + 2 * STEPS,)),
                dma((RING + 2 * STEPS,)),
                dma((3 * (UPLV + 1),)),
                dma((3 * (UPLV + 1),)),
            ],
            compiler_params=pltpu.CompilerParams(
                collective_id=0, has_side_effects=True, vmem_limit_bytes=56 * 2**20
            ),
        )(
            light,
            probes,
            near_list.T,
            far_list,
            jnp.swapaxes(leaf_basis, 1, 2),
            leaf_transfer.reshape(LEAVES * RANK, RANK),
            far_coupling.reshape(LEAVES, NFAR * RANK, RANK),
            up_transfer,
            upper_coupling,
        )

    return jax.shard_map(
        per_device,
        mesh=mesh,
        in_specs=(
            P(None, ("leaf", "sub")),
            P(None, ("leaf", "sub")),
            P(("leaf", "sub"), None),
            P(("leaf", "sub"), None),
            P(("leaf", "sub"), None, None),
            P(("leaf", "sub"), None, None),
            P(("leaf", "sub"), None, None, None),
            P(),
            P(),
        ),
        out_specs=P(None, ("leaf", "sub")),
        check_vma=False,
    )
```

```python
import functools

import jax
import jax.numpy as jnp
from jax import lax
from jax.experimental import pallas as pl
from jax.experimental.pallas import tpu as pltpu
from jax.sharding import PartitionSpec as P

MESH = pl.DeviceIdType.MESH
F32, BF16 = jnp.float32, jnp.bfloat16

HALO = 4
UPLV = 3
LEAF = 256
RANK = 64
LIGHTS = 32
LEAVES = 8
NNEAR = 4
NFAR = 32
soften = 0.0025
spacing = 0.25

RING = 8
LINE = RING * RING
PER_CHIP = 4
STEPS = RING * RING // 2
WHOLE = 16
HALVES = 24

NEAREST = (0, -1, 1, -2, 2)

NT = (((1,), (1,)), ((), ()))


def offset_of(j):
    return ((j + 1) // 2) * (1 - 2 * (j % 2))


def kernel(
    devices,
    light_hbm,
    probes_ref,
    near_list_ref,
    far_list_ref,
    basis_hbm,
    transfer_hbm,
    coupling_hbm,
    up_ref,
    upper_ref,
    out_ref,
    window,
    geo,
    columns,
    basis,
    transfer,
    coupling,
    pool,
    traded,
    near_terms,
    pulled,
    tile,
    upward,
    mine,
    partner,
    below,
    above,
    mask,
    load_sem,
    halo_send,
    halo_recv,
    first_send,
    first_recv,
    right_send,
    right_recv,
    left_send,
    left_recv,
    sib_send,
    sib_recv,
    tree_send,
    tree_recv,
):
    leaf = lax.axis_index("leaf")
    sub = lax.axis_index("sub")
    me = leaf * 4 + sub
    core = leaf % 2
    y = (leaf // 2) % RING
    z = leaf // (2 * RING)
    first = y + core * (z - y)
    second = z + core * (y - z)

    def device(index):
        index = lax.rem(index + devices, devices)
        return (index // 4, lax.rem(index, 4))

    def chip(a, b):
        a = lax.rem(a + RING, RING)
        b = lax.rem(b + RING, RING)
        row = a + core * (b - a)
        layer = b + core * (a - b)
        return ((layer * RING + row) * 2 + core, sub)

    def across(a, b):
        to_leaf, to_sub = chip(a, b)
        return (to_leaf + 1 - 2 * core, to_sub)

    right, left = chip(first, second + 1), chip(first, second - 1)
    sibling = (leaf + 1 - 2 * core, sub)

    def load(source, target, index):
        copy = pltpu.make_async_copy(source, target, load_sem.at[index])
        copy.start()
        return copy

    light_loads = [
        load(light_hbm.at[:, pl.ds(t * LEAF, LEAF)], window.at[HALO + t], 4 + t) for t in range(LEAVES)
    ]
    basis_load = load(basis_hbm, basis, 1)
    transfer_load = load(transfer_hbm, transfer, 2)
    coupling_load = load(coupling_hbm, coupling, 3)

    barrier = pltpu.get_barrier_semaphore()
    friends = [device(me + s * k) for k in (1, 2, 4, 8, 16) for s in (1, -1)]
    friends += [right, left]
    friends += [chip(first + k, second) for k in NEAREST if k]
    friends += [across(first + k, second) for k in NEAREST]
    for friend in friends:
        pl.semaphore_signal(barrier, inc=1, device_id=friend, device_id_type=MESH)

    geo[HALO : HALO + LEAVES] = jnp.zeros((LEAVES, 8, LEAF), F32)
    for t in range(LEAVES):
        geo[HALO + t, 0:4, :] = probes_ref[:, t * LEAF : (t + 1) * LEAF].astype(F32)
    lanes = lax.broadcasted_iota(jnp.int32, (LIGHTS, 2 * RANK), 1)
    mask[0] = jnp.where(lanes < RANK, 1.0, 0.0).astype(BF16)
    mask[1] = jnp.where(lanes < RANK, 0.0, 1.0).astype(BF16)

    def send(source, target, send_sem, recv_sem, to):
        return pltpu.make_async_remote_copy(
            src_ref=source,
            dst_ref=target,
            send_sem=send_sem,
            recv_sem=recv_sem,
            device_id=to,
            device_id_type=MESH,
        )

    def halo(ref, index):
        down = send(
            ref.at[pl.ds(HALO, HALO)],
            ref.at[pl.ds(HALO + LEAVES, HALO)],
            halo_send.at[index],
            halo_recv.at[index],
            device(me - 1),
        )
        up = send(
            ref.at[pl.ds(LEAVES, HALO)],
            ref.at[pl.ds(0, HALO)],
            halo_send.at[index + 1],
            halo_recv.at[index + 1],
            device(me + 1),
        )
        down.start()
        up.start()
        return [down, up]

    for light_load in light_loads:
        light_load.wait()
    basis_load.wait()

    chip_place = z * RING + y
    my_block = (core * LINE + chip_place) * PER_CHIP
    pairs = []
    for q in range(LEAVES // 2):
        parts = []
        for t in (2 * q, 2 * q + 1):
            parts.append(lax.dot_general(window[HALO + t], basis[t], NT, preferred_element_type=F32))
        pairs.append(jnp.concatenate(parts, axis=1).astype(BF16))
    for i in range(2):
        lower, higher = pairs[i], pairs[2 + i]
        pool[my_block + core * 2 + i] = jnp.where(core == 0, lower.astype(F32), higher.astype(F32)).astype(BF16)
        traded[i] = jnp.where(core == 0, higher.astype(F32), lower.astype(F32)).astype(BF16)
    other_block = ((1 - core) * LINE + chip_place) * PER_CHIP

    pl.semaphore_wait(barrier, len(friends))

    for j, k in enumerate(NEAREST):
        theirs = pool.at[pl.ds(other_block + core * 2, 2)]
        send(traded, theirs, first_send, first_recv.at[j], across(first, second - k)).start()
        if k:
            ours = pool.at[pl.ds(my_block + core * 2, 2)]
            send(ours, ours, first_send, first_recv.at[j], chip(first - k, second)).start()
    halos = halo(geo, 0) + halo(window, 2)

    transfer_load.wait()
    stacked = jnp.concatenate(pairs, axis=1)
    level0 = jnp.dot(stacked, transfer[...], preferred_element_type=F32)

    def twice(value):
        return jnp.concatenate([value, value], axis=1)

    def exact(value, matrix, dims=(((1,), (0,)), ((), ()))):
        high = value.astype(BF16)
        rest = value - high.astype(F32)
        middle = rest.astype(BF16)
        low = (rest - middle.astype(F32)).astype(BF16)
        parts = jnp.concatenate([high, middle, low], axis=0)
        product = lax.dot_general(parts, matrix, dims, preferred_element_type=F32)
        return product[:LIGHTS] + (product[LIGHTS : 2 * LIGHTS] + product[2 * LIGHTS :])

    def climb(height, value):
        upward[height] = twice(value)
        stride = 2 ** (height + 1)
        moves = [
            send(
                upward.at[height],
                below.at[height],
                tree_send.at[3 * height],
                tree_recv.at[3 * height],
                device(me + stride),
            ),
            send(
                upward.at[height],
                above.at[height],
                tree_send.at[3 * height + 1],
                tree_recv.at[3 * height + 1],
                device(me - stride),
            ),
        ]
        if height < UPLV:
            parity = (me // 2**height) % 2
            mine[height] = twice(exact(value, up_ref[height, parity]))
            swap = send(
                mine.at[height],
                partner.at[height],
                tree_send.at[3 * height + 2],
                tree_recv.at[3 * height + 2],
                device(me + (1 - 2 * parity) * 2**height),
            )
            swap.start()
            moves.append(swap)
        moves[0].start()
        moves[1].start()
        return moves

    tree = [climb(0, level0)]

    half_base = core * LINE

    def block(a, b, count=PER_CHIP, skip=0):
        a = lax.rem(a + 2 * RING, RING)
        b = lax.rem(b + 2 * RING, RING)
        row, layer = a + core * (b - a), b + core * (a - b)
        return pool.at[pl.ds((half_base + layer * RING + row) * PER_CHIP + skip, count)]

    def to_second(j):
        ref = block(first + offset_of(j), second)
        for send_sem, recv_sem, to in (
            (right_send, right_recv, right),
            (left_send, left_recv, left),
        ):
            send(ref, ref, send_sem, recv_sem.at[j], to).start()
        send(ref, ref, sib_send, sib_recv, sibling).start()

    def arrive(j):
        ref = block(first + offset_of(j), second)
        if j == 0:
            ref = block(first, second, 2)
        send(ref, ref, first_send, first_recv.at[j], sibling).wait_recv()

    def pass_on(j, later, to):
        ref = block(first + offset_of(j), second)
        send(ref, ref, first_send, first_recv.at[later], to).start()

    def spread_columns(t):
        turned = jnp.transpose(geo[HALO + t])
        for k in range(4):
            value = turned[:, k : k + 1]
            if k == 3:
                value = value * soften
            columns[t, k] = jnp.broadcast_to(value, (LEAF, 128))

    def add_tile(t, w, shift, before):
        rows = geo[w]
        row_x, row_y, row_z, row_a = (rows[0:1] - shift, rows[1:2], rows[2:3], rows[3:4])
        for i in range(0, LEAF, 32):
            sides = []
            for lane in (0, 128):
                cut = slice(lane, lane + 128)
                dx = columns[t, 0, i : i + 32] - row_x[:, cut]
                dy = columns[t, 1, i : i + 32] - row_y[:, cut]
                dz = columns[t, 2, i : i + 32] - row_z[:, cut]
                total = dx * dx + soften + dy * dy + dz * dz
                guess = pl.reciprocal(total, approx=True)
                guess = guess * (2.0 - total * guess)
                sides.append((columns[t, 3, i : i + 32] * row_a[:, cut] * guess).astype(BF16))
            tile[i : i + 32, :] = jnp.concatenate(sides, axis=1)
        near_terms[t] = before + lax.dot_general(window[w], tile[...], NT, preferred_element_type=F32)

    def near_self(t, carry):
        add_tile(t, HALO + t, 0.0, 0.0)
        return carry

    def near_pair(p):
        t, k = p // NNEAR, p % NNEAR
        w = (near_list_ref[k, t] - LEAVES * me + HALO) & (LEAVES + 2 * HALO - 1)
        add_tile(t, w, (t + HALO - w).astype(F32) * spacing, near_terms[t])

    for t in range(LEAVES):
        spread_columns(t)

    for j in range(5):
        arrive(j)
        if j == 3:
            pass_on(3, 5, chip(first + 1, second))
            pass_on(3, 7, chip(first + 2, second))
        if j == 4:
            pass_on(4, 6, chip(first - 1, second))
        to_second(j)
    lax.fori_loop(0, LEAVES // 2, near_self, 0)
    for j in range(5, RING):
        arrive(j)
        to_second(j)
    lax.fori_loop(LEAVES // 2, LEAVES, near_self, 0)

    def rejoin(height):
        tree[height][2].wait_recv()
        total = mine[height] + partner[height]
        tree.append(climb(height + 1, total[:, :RANK]))

    for move in halos:
        move.wait_recv()

    sides = (
        (1, right, right_send, right_recv, 0),
        (-1, left, left_send, left_recv, 2),
    )

    def whole_step(n, carry):
        for sign, to, send_sem, recv_sem, skip in sides:
            ref = block(first + offset_of(n % RING), second - sign * (n // RING + 1))
            send(ref, ref, send_sem, recv_sem.at[n], to).wait_recv()
            send(ref, ref, send_sem, recv_sem.at[n + RING], to).start()
            send(ref, ref, sib_send, sib_recv, sibling).start()
        near_pair(n)
        return carry

    def half_step(n, carry):
        for sign, to, send_sem, recv_sem, skip in sides:
            a, b = first + offset_of(n % RING), second - sign * (n // RING + 1)
            ref, part = block(a, b), block(a, b, 2, skip)
            send(ref, ref, send_sem, recv_sem.at[n], to).wait_recv()
            send(part, part, send_sem, recv_sem.at[n + RING], to).start()
            send(ref, ref, sib_send, sib_recv, sibling).start()
        near_pair(n)
        return carry

    def last_step(n, carry):
        for sign, to, send_sem, recv_sem, skip in sides:
            a, b = first + offset_of(n % RING), second - sign * (n // RING + 1)
            part = block(a, b, 2, skip)
            send(part, part, send_sem, recv_sem.at[n], to).wait_recv()
            send(part, part, sib_send, sib_recv, sibling).start()
        near_pair(n)
        return carry

    done = 0
    for height in range(UPLV):
        lax.fori_loop(done, 4 * height + 2, whole_step, 0)
        done = 4 * height + 2
        rejoin(height)
    lax.fori_loop(done, WHOLE, whole_step, 0)
    lax.fori_loop(WHOLE, HALVES, half_step, 0)

    downward = None
    for height in range(UPLV, -1, -1):
        tree[height][0].wait_recv()
        tree[height][1].wait_recv()
        cluster = me // 2**height
        low = jnp.where(cluster >= 2, below[height][:, :RANK], 0.0)
        high = jnp.where(cluster + 2 < devices // 2**height, above[height][:, :RANK], 0.0)
        value = exact(low, upper_ref[height, 0]) + exact(high, upper_ref[height, 1])
        if downward is not None:
            value += exact(downward, up_ref[height, cluster % 2], NT)
        downward = value
    pulled[...] = exact(downward, transfer[...], NT)

    lax.fori_loop(HALVES, STEPS, last_step, 0)

    coupling_load.wait()

    others = pool.at[pl.ds((1 - core) * LINE * PER_CHIP, LINE * PER_CHIP)]
    send(others, others, sib_send, sib_recv, sibling).wait_recv()

    for t in range(LEAVES):
        picked, weights = [], []
        for c in range(NFAR):
            entry = far_list_ref[t, c]
            group, peer, pair = (entry >> 2) & 1, entry >> 5, (entry >> 1) & 1
            picked.append(pool[group * (LINE * PER_CHIP) + peer * 2 + pair] * mask[entry & 1])
            cut = coupling[t, c * RANK : (c + 1) * RANK, :]
            weights += [cut, cut]
        far = jnp.dot(
            jnp.concatenate(picked, axis=1),
            jnp.concatenate(weights, axis=0),
            preferred_element_type=F32,
        )
        leaf_far = (far + pulled[:, t * RANK : (t + 1) * RANK]).astype(BF16)
        back = jnp.dot(leaf_far, basis[t], preferred_element_type=F32)
        out_ref[:, t * LEAF : (t + 1) * LEAF] = (near_terms[t] + back).astype(BF16)

    for move in halos + [m for moves in tree for m in moves]:
        move.wait_send()

    def sent(count, send_sem):
        ref = pool.at[pl.ds(0, count)]
        send(ref, ref, send_sem, sib_recv, sibling).wait_send()

    sent(2 * (2 * len(NEAREST) - 1) + 3 * PER_CHIP, first_send)
    sent(HALVES * PER_CHIP + (STEPS - HALVES) * 2, right_send)
    sent(HALVES * PER_CHIP + (STEPS - HALVES) * 2, left_send)
    sent(LINE * PER_CHIP, sib_send)


def solution(mesh):
    devices = mesh.shape["leaf"] * mesh.shape["sub"]

    def per_device(
        light,
        probes,
        near_list,
        far_list,
        leaf_basis,
        leaf_transfer,
        far_coupling,
        up_transfer,
        upper_coupling,
    ):
        any_space = pl.BlockSpec(memory_space=pl.ANY)
        vmem = pl.BlockSpec(memory_space=pltpu.VMEM)
        smem = pl.BlockSpec(memory_space=pltpu.SMEM)
        dma = pltpu.SemaphoreType.DMA
        slots = LEAVES + 2 * HALO
        return pl.pallas_call(
            functools.partial(kernel, devices),
            out_shape=jax.ShapeDtypeStruct((LIGHTS, LEAVES * LEAF), BF16),
            in_specs=[any_space, vmem, smem, smem, any_space, any_space, any_space, vmem, vmem],
            out_specs=vmem,
            scratch_shapes=[
                pltpu.VMEM((slots, LIGHTS, LEAF), BF16),
                pltpu.VMEM((slots, 8, LEAF), F32),
                pltpu.VMEM((LEAVES, 4, LEAF, 128), F32),
                pltpu.VMEM((LEAVES, RANK, LEAF), BF16),
                pltpu.VMEM((LEAVES * RANK, RANK), BF16),
                pltpu.VMEM((LEAVES, NFAR * RANK, RANK), BF16),
                pltpu.VMEM((2 * LINE * PER_CHIP, LIGHTS, 2 * RANK), BF16),
                pltpu.VMEM((2, LIGHTS, 2 * RANK), BF16),
                pltpu.VMEM((LEAVES, LIGHTS, LEAF), F32),
                pltpu.VMEM((LIGHTS, LEAVES * RANK), F32),
                pltpu.VMEM((LEAF, LEAF), BF16),
                pltpu.VMEM((UPLV + 1, LIGHTS, 2 * RANK), F32),
                pltpu.VMEM((UPLV, LIGHTS, 2 * RANK), F32),
                pltpu.VMEM((UPLV, LIGHTS, 2 * RANK), F32),
                pltpu.VMEM((UPLV + 1, LIGHTS, 2 * RANK), F32),
                pltpu.VMEM((UPLV + 1, LIGHTS, 2 * RANK), F32),
                pltpu.VMEM((2, LIGHTS, 2 * RANK), BF16),
                dma((4 + LEAVES,)),
                dma((4,)),
                dma((4,)),
                dma,
                dma((RING,)),
                dma,
                dma((STEPS,)),
                dma,
                dma((STEPS,)),
                dma,
                dma,
                dma((3 * (UPLV + 1),)),
                dma((3 * (UPLV + 1),)),
            ],
            compiler_params=pltpu.CompilerParams(
                collective_id=0, has_side_effects=True, vmem_limit_bytes=56 * 2**20
            ),
        )(
            light,
            probes,
            near_list.T,
            far_list,
            jnp.swapaxes(leaf_basis, 1, 2),
            leaf_transfer.reshape(LEAVES * RANK, RANK),
            far_coupling.reshape(LEAVES, NFAR * RANK, RANK),
            up_transfer,
            upper_coupling,
        )

    return jax.shard_map(
        per_device,
        mesh=mesh,
        in_specs=(
            P(None, ("leaf", "sub")),
            P(None, ("leaf", "sub")),
            P(("leaf", "sub"), None),
            P(("leaf", "sub"), None),
            P(("leaf", "sub"), None, None),
            P(("leaf", "sub"), None, None),
            P(("leaf", "sub"), None, None, None),
            P(),
            P(),
        ),
        out_specs=P(None, ("leaf", "sub")),
        check_vma=False,
    )
```

```python
import functools

import jax
import jax.numpy as jnp
from jax import lax
from jax.experimental import pallas as pl
from jax.experimental.pallas import tpu as pltpu
from jax.sharding import PartitionSpec as P

MESH = pl.DeviceIdType.MESH
F32, BF16 = jnp.float32, jnp.bfloat16

HALO = 4
UPLV = 3
LEAF = 256
RANK = 64
LIGHTS = 32
LEAVES = 8
NNEAR = 4
NFAR = 32
soften = 0.0025
spacing = 0.25

RING = 8
LINE = RING * RING
PER_CHIP = 4
CHUNKS = 4
CHUNK = RING // CHUNKS * PER_CHIP
STEPS = RING // 2 * CHUNKS - CHUNKS // 2
PASSED = STEPS - CHUNKS
TILES = 3

NT = (((1,), (1,)), ((), ()))


def kernel(
    devices,
    light_hbm,
    probes_ref,
    near_list_ref,
    far_list_ref,
    basis_hbm,
    transfer_hbm,
    coupling_hbm,
    up_ref,
    upper_ref,
    out_ref,
    window,
    geo,
    columns,
    basis,
    transfer,
    coupling,
    pool,
    traded,
    near_terms,
    pulled,
    tile,
    upward,
    mine,
    partner,
    below,
    above,
    mask,
    codes,
    load_sem,
    halo_send,
    halo_recv,
    first_send,
    first_recv,
    right_send,
    right_recv,
    left_send,
    left_recv,
    sib_send,
    sib_recv,
    tree_send,
    tree_recv,
):
    leaf = lax.axis_index("leaf")
    sub = lax.axis_index("sub")
    me = leaf * 4 + sub
    core = leaf % 2
    y = (leaf // 2) % RING
    z = leaf // (2 * RING)
    first = y + core * (z - y)
    second = z + core * (y - z)

    def device(index):
        index = lax.rem(index + devices, devices)
        return (index // 4, lax.rem(index, 4))

    def chip(a, b):
        a = lax.rem(a + RING, RING)
        b = lax.rem(b + RING, RING)
        row = a + core * (b - a)
        layer = b + core * (a - b)
        return ((layer * RING + row) * 2 + core, sub)

    def across(a, b):
        to_leaf, to_sub = chip(a, b)
        return (to_leaf + 1 - 2 * core, to_sub)

    right, left = chip(first, second + 1), chip(first, second - 1)
    sibling = (leaf + 1 - 2 * core, sub)

    def load(source, target, index):
        copy = pltpu.make_async_copy(source, target, load_sem.at[index])
        copy.start()
        return copy

    light_loads = [
        load(light_hbm.at[:, pl.ds(t * LEAF, LEAF)], window.at[HALO + t], 4 + t) for t in range(LEAVES)
    ]
    basis_load = load(basis_hbm, basis, 1)
    transfer_load = load(transfer_hbm, transfer, 2)
    coupling_load = load(coupling_hbm, coupling, 3)

    barrier = pltpu.get_barrier_semaphore()
    friends = [device(me + s * k) for k in (1, 2, 4, 8, 16) for s in (1, -1)]
    friends += [right, left]
    friends += [chip(first + k, second) for k in range(1, RING)]
    friends += [across(first + k, second) for k in range(RING)]
    for friend in friends:
        pl.semaphore_signal(barrier, inc=1, device_id=friend, device_id_type=MESH)

    geo[HALO : HALO + LEAVES] = jnp.zeros((LEAVES, 8, LEAF), F32)
    for t in range(LEAVES):
        geo[HALO + t, 0:4, :] = probes_ref[:, t * LEAF : (t + 1) * LEAF].astype(F32)
    lanes = lax.broadcasted_iota(jnp.int32, (LIGHTS, 2 * RANK), 1)
    mask[0] = jnp.where(lanes < RANK, 1.0, 0.0).astype(BF16)
    mask[1] = jnp.where(lanes < RANK, 0.0, 1.0).astype(BF16)

    def send(source, target, send_sem, recv_sem, to):
        return pltpu.make_async_remote_copy(
            src_ref=source,
            dst_ref=target,
            send_sem=send_sem,
            recv_sem=recv_sem,
            device_id=to,
            device_id_type=MESH,
        )

    def halo(ref, index):
        down = send(
            ref.at[pl.ds(HALO, HALO)],
            ref.at[pl.ds(HALO + LEAVES, HALO)],
            halo_send.at[index],
            halo_recv.at[index],
            device(me - 1),
        )
        up = send(
            ref.at[pl.ds(LEAVES, HALO)],
            ref.at[pl.ds(0, HALO)],
            halo_send.at[index + 1],
            halo_recv.at[index + 1],
            device(me + 1),
        )
        down.start()
        up.start()
        return [down, up]

    for light_load in light_loads:
        light_load.wait()
    basis_load.wait()

    my_block = (core * LINE + second * RING + first) * PER_CHIP + core * 2
    pairs = []
    for q in range(LEAVES // 2):
        parts = []
        for t in (2 * q, 2 * q + 1):
            parts.append(lax.dot_general(window[HALO + t], basis[t], NT, preferred_element_type=F32))
        pairs.append(jnp.concatenate(parts, axis=1).astype(BF16))
    for i in range(2):
        lower, higher = pairs[i], pairs[2 + i]
        pool[my_block + i] = jnp.where(core == 0, lower.astype(F32), higher.astype(F32)).astype(BF16)
        traded[i] = jnp.where(core == 0, higher.astype(F32), lower.astype(F32)).astype(BF16)
    other_block = ((1 - core) * LINE + first * RING + second) * PER_CHIP + core * 2

    pl.semaphore_wait(barrier, len(friends))

    ours, theirs = pool.at[pl.ds(my_block, 2)], pool.at[pl.ds(other_block, 2)]
    for k in range(RING):
        send(traded, theirs, first_send, first_recv.at[second // 2], across(first, second + k)).start()
        if k:
            send(ours, ours, first_send, first_recv.at[first // 2], chip(first + k, second)).start()
    halos = halo(geo, 0) + halo(window, 2)

    transfer_load.wait()
    stacked = jnp.concatenate(pairs, axis=1)
    level0 = jnp.dot(stacked, transfer[...], preferred_element_type=F32)

    def twice(value):
        return jnp.concatenate([value, value], axis=1)

    def exact(value, matrix, dims=(((1,), (0,)), ((), ()))):
        high = value.astype(BF16)
        rest = value - high.astype(F32)
        middle = rest.astype(BF16)
        low = (rest - middle.astype(F32)).astype(BF16)
        parts = jnp.concatenate([high, middle, low], axis=0)
        product = lax.dot_general(parts, matrix, dims, preferred_element_type=F32)
        return product[:LIGHTS] + (product[LIGHTS : 2 * LIGHTS] + product[2 * LIGHTS :])

    def climb(height, value):
        upward[height] = twice(value)
        stride = 2 ** (height + 1)
        moves = [
            send(
                upward.at[height],
                below.at[height],
                tree_send.at[3 * height],
                tree_recv.at[3 * height],
                device(me + stride),
            ),
            send(
                upward.at[height],
                above.at[height],
                tree_send.at[3 * height + 1],
                tree_recv.at[3 * height + 1],
                device(me - stride),
            ),
        ]
        if height < UPLV:
            parity = (me // 2**height) % 2
            mine[height] = twice(exact(value, up_ref[height, parity]))
            swap = send(
                mine.at[height],
                partner.at[height],
                tree_send.at[3 * height + 2],
                tree_recv.at[3 * height + 2],
                device(me + (1 - 2 * parity) * 2**height),
            )
            swap.start()
            moves.append(swap)
        moves[0].start()
        moves[1].start()
        return moves

    tree = [climb(0, level0)]

    def chunk(n, sign):
        b = lax.rem(second - sign * (n // CHUNKS) + RING, RING)
        q = lax.rem(first // 2 + n + (CHUNKS // 2) * (sign < 0) + 2 * RING, CHUNKS)
        return pool.at[pl.ds((core * LINE + b * RING) * PER_CHIP + q * CHUNK, CHUNK)]

    def arrive(q):
        at = lax.rem(first // 2 + q, CHUNKS)
        ref = pool.at[pl.ds(0, CHUNK if q else CHUNK - 2)]
        send(ref, ref, first_send, first_recv.at[at], sibling).wait_recv()

    def to_right(n):
        ref = chunk(n, 1)
        send(ref, ref, right_send, right_recv.at[n], right).start()

    def to_left(n):
        ref = chunk(n, -1)
        send(ref, ref, left_send, left_recv.at[n], left).start()

    def to_sibling(ref):
        send(ref, ref, sib_send, sib_recv, sibling).start()

    def spread_columns(t):
        turned = jnp.transpose(geo[HALO + t])
        for k in range(4):
            value = turned[:, k : k + 1]
            if k == 3:
                value = value * soften
            columns[t, k] = jnp.broadcast_to(value, (LEAF, 128))

    def add_tile(t, w, shift, before, slot):
        rows = geo[w]
        row_x, row_y, row_z, row_a = (rows[0:1] - shift, rows[1:2], rows[2:3], rows[3:4])
        for i in range(0, LEAF, 32):
            sides = []
            for lane in (0, 128):
                cut = slice(lane, lane + 128)
                dx = columns[t, 0, i : i + 32] - row_x[:, cut]
                dy = columns[t, 1, i : i + 32] - row_y[:, cut]
                dz = columns[t, 2, i : i + 32] - row_z[:, cut]
                total = dx * dx + soften + dy * dy + dz * dz
                guess = pl.reciprocal(total, approx=True)
                guess = guess * (2.0 - total * guess)
                sides.append((columns[t, 3, i : i + 32] * row_a[:, cut] * guess).astype(BF16))
            tile[slot, i : i + 32, :] = jnp.concatenate(sides, axis=1)
        near_terms[t] = before + lax.dot_general(window[w], tile[slot], NT, preferred_element_type=F32)

    def near_pair(p, slot):
        t, k = p // NNEAR, p % NNEAR
        w = (near_list_ref[k, t] - LEAVES * me + HALO) & (LEAVES + 2 * HALO - 1)
        add_tile(t, w, (t + HALO - w).astype(F32) * spacing, near_terms[t], slot)

    def encode(t, carry):
        for c in range(NFAR):
            entry = far_list_ref[t, c]
            layer, row, group = entry >> 9, (entry >> 6) & 7, (entry >> 2) & 1
            low, high = layer * RING + row, row * RING + layer + LINE
            place = low + group * (high - low)
            codes[t, c] = place * 8 + ((entry >> 5) & 1) * 4 + (entry & 3)
        return carry

    for t in range(LEAVES):
        spread_columns(t)
    lax.fori_loop(0, LEAVES, encode, 0)
    for t in range(LEAVES // 2):
        add_tile(t, HALO + t, 0.0, 0.0, t % TILES)

    arrive(0)
    to_right(0)
    arrive(2)
    to_left(0)
    arrive(1)
    to_right(1)
    arrive(3)
    to_left(1)
    for n in (2, 3):
        to_right(n)
        to_left(n)
    for n in range(CHUNKS):
        to_sibling(chunk(n, 1))
    for t in range(LEAVES // 2, LEAVES):
        add_tile(t, HALO + t, 0.0, 0.0, t % TILES)

    def rejoin(height):
        tree[height][2].wait_recv()
        total = mine[height] + partner[height]
        tree.append(climb(height + 1, total[:, :RANK]))

    for move in halos:
        move.wait_recv()

    def pass_step(n, carry):
        ref = chunk(n + CHUNKS, 1)
        send(ref, ref, right_send, right_recv.at[n], right).wait_recv()
        send(ref, ref, right_send, right_recv.at[n + CHUNKS], right).start()
        ref_left = chunk(n + CHUNKS, -1)
        send(ref_left, ref_left, left_send, left_recv.at[n], left).wait_recv()
        send(ref_left, ref_left, left_send, left_recv.at[n + CHUNKS], left).start()
        to_sibling(ref)
        to_sibling(ref_left)
        for i in range(TILES):
            near_pair(TILES * n + i, i)
        return carry

    def last_step(n, carry):
        ref = chunk(n + CHUNKS, 1)
        send(ref, ref, right_send, right_recv.at[n], right).wait_recv()
        to_sibling(ref)
        ref_left = chunk(n + CHUNKS, -1)
        send(ref_left, ref_left, left_send, left_recv.at[n], left).wait_recv()
        to_sibling(ref_left)
        return carry

    done = 0
    for height in range(UPLV):
        lax.fori_loop(done, 3 * height + 2, pass_step, 0)
        done = 3 * height + 2
        rejoin(height)
    lax.fori_loop(done, PASSED, pass_step, 0)
    for p in range(TILES * PASSED, LEAVES * NNEAR):
        near_pair(p, p % TILES)

    downward = None
    for height in range(UPLV, -1, -1):
        tree[height][0].wait_recv()
        tree[height][1].wait_recv()
        cluster = me // 2**height
        low = jnp.where(cluster >= 2, below[height][:, :RANK], 0.0)
        high = jnp.where(cluster + 2 < devices // 2**height, above[height][:, :RANK], 0.0)
        value = exact(low, upper_ref[height, 0]) + exact(high, upper_ref[height, 1])
        if downward is not None:
            value += exact(downward, up_ref[height, cluster % 2], NT)
        downward = value
    pulled[...] = exact(downward, transfer[...], NT)

    lax.fori_loop(PASSED, STEPS, last_step, 0)

    coupling_load.wait()

    others = pool.at[pl.ds((1 - core) * LINE * PER_CHIP, LINE * PER_CHIP)]
    send(others, others, sib_send, sib_recv, sibling).wait_recv()

    for t in range(LEAVES):
        picked, weights = [], []
        for c in range(NFAR):
            code = codes[t, c]
            picked.append(pool[code >> 1] * mask[code & 1])
            cut = coupling[t, c * RANK : (c + 1) * RANK, :]
            weights += [cut, cut]
        far = jnp.dot(
            jnp.concatenate(picked, axis=1),
            jnp.concatenate(weights, axis=0),
            preferred_element_type=F32,
        )
        leaf_far = (far + pulled[:, t * RANK : (t + 1) * RANK]).astype(BF16)
        back = jnp.dot(leaf_far, basis[t], preferred_element_type=F32)
        out_ref[:, t * LEAF : (t + 1) * LEAF] = (near_terms[t] + back).astype(BF16)

    for move in halos + [m for moves in tree for m in moves]:
        move.wait_send()

    def sent(count, send_sem):
        ref = pool.at[pl.ds(0, count)]
        send(ref, ref, send_sem, sib_recv, sibling).wait_send()

    sent(2 * (2 * RING - 1), first_send)
    sent(STEPS * CHUNK, right_send)
    sent(STEPS * CHUNK, left_send)
    sent(LINE * PER_CHIP, sib_send)


def solution(mesh):
    devices = mesh.shape["leaf"] * mesh.shape["sub"]

    def per_device(
        light,
        probes,
        near_list,
        far_list,
        leaf_basis,
        leaf_transfer,
        far_coupling,
        up_transfer,
        upper_coupling,
    ):
        any_space = pl.BlockSpec(memory_space=pl.ANY)
        vmem = pl.BlockSpec(memory_space=pltpu.VMEM)
        smem = pl.BlockSpec(memory_space=pltpu.SMEM)
        dma = pltpu.SemaphoreType.DMA
        slots = LEAVES + 2 * HALO
        return pl.pallas_call(
            functools.partial(kernel, devices),
            out_shape=jax.ShapeDtypeStruct((LIGHTS, LEAVES * LEAF), BF16),
            in_specs=[any_space, vmem, smem, smem, any_space, any_space, any_space, vmem, vmem],
            out_specs=vmem,
            scratch_shapes=[
                pltpu.VMEM((slots, LIGHTS, LEAF), BF16),
                pltpu.VMEM((slots, 8, LEAF), F32),
                pltpu.VMEM((LEAVES, 4, LEAF, 128), F32),
                pltpu.VMEM((LEAVES, RANK, LEAF), BF16),
                pltpu.VMEM((LEAVES * RANK, RANK), BF16),
                pltpu.VMEM((LEAVES, NFAR * RANK, RANK), BF16),
                pltpu.VMEM((2 * LINE * PER_CHIP, LIGHTS, 2 * RANK), BF16),
                pltpu.VMEM((2, LIGHTS, 2 * RANK), BF16),
                pltpu.VMEM((LEAVES, LIGHTS, LEAF), F32),
                pltpu.VMEM((LIGHTS, LEAVES * RANK), F32),
                pltpu.VMEM((TILES, LEAF, LEAF), BF16),
                pltpu.VMEM((UPLV + 1, LIGHTS, 2 * RANK), F32),
                pltpu.VMEM((UPLV, LIGHTS, 2 * RANK), F32),
                pltpu.VMEM((UPLV, LIGHTS, 2 * RANK), F32),
                pltpu.VMEM((UPLV + 1, LIGHTS, 2 * RANK), F32),
                pltpu.VMEM((UPLV + 1, LIGHTS, 2 * RANK), F32),
                pltpu.VMEM((2, LIGHTS, 2 * RANK), BF16),
                pltpu.SMEM((LEAVES, NFAR), jnp.int32),
                dma((4 + LEAVES,)),
                dma((4,)),
                dma((4,)),
                dma,
                dma((CHUNKS,)),
                dma,
                dma((STEPS,)),
                dma,
                dma((STEPS,)),
                dma,
                dma,
                dma((3 * (UPLV + 1),)),
                dma((3 * (UPLV + 1),)),
            ],
            compiler_params=pltpu.CompilerParams(
                collective_id=0, has_side_effects=True, vmem_limit_bytes=56 * 2**20
            ),
        )(
            light,
            probes,
            near_list.T,
            far_list,
            jnp.swapaxes(leaf_basis, 1, 2),
            leaf_transfer.reshape(LEAVES * RANK, RANK),
            far_coupling.reshape(LEAVES, NFAR * RANK, RANK),
            up_transfer,
            upper_coupling,
        )

    return jax.shard_map(
        per_device,
        mesh=mesh,
        in_specs=(
            P(None, ("leaf", "sub")),
            P(None, ("leaf", "sub")),
            P(("leaf", "sub"), None),
            P(("leaf", "sub"), None),
            P(("leaf", "sub"), None, None),
            P(("leaf", "sub"), None, None),
            P(("leaf", "sub"), None, None, None),
            P(),
            P(),
        ),
        out_specs=P(None, ("leaf", "sub")),
        check_vma=False,
    )
```

```python
import functools

import jax
import jax.numpy as jnp
from jax import lax
from jax.experimental import pallas as pl
from jax.experimental.pallas import tpu as pltpu
from jax.sharding import PartitionSpec as P

MESH = pl.DeviceIdType.MESH
F32, BF16 = jnp.float32, jnp.bfloat16

HALO = 4
UPLV = 3
LEAF = 256
RANK = 64
LIGHTS = 32
LEAVES = 8
NNEAR = 4
NFAR = 32
soften = 0.0025
spacing = 0.25

RING = 8
LINE = RING * RING
PER_CHIP = 4
CHUNKS = 4
CHUNK = RING // CHUNKS * PER_CHIP
STEPS = RING // 2 * CHUNKS - CHUNKS // 2
TILES = 3

NT = (((1,), (1,)), ((), ()))


def kernel(
    devices,
    light_hbm,
    probes_ref,
    near_list_ref,
    far_list_ref,
    basis_hbm,
    transfer_hbm,
    coupling_hbm,
    up_ref,
    upper_ref,
    out_ref,
    window,
    geo,
    columns,
    basis,
    transfer,
    coupling,
    pool,
    traded,
    near_terms,
    pulled,
    tile,
    upward,
    mine,
    partner,
    below,
    above,
    mask,
    codes,
    load_sem,
    halo_send,
    halo_recv,
    first_send,
    first_recv,
    right_send,
    right_recv,
    left_send,
    left_recv,
    sib_send,
    sib_recv,
    tree_send,
    tree_recv,
):
    leaf = lax.axis_index("leaf")
    sub = lax.axis_index("sub")
    me = leaf * 4 + sub
    core = leaf % 2
    y = (leaf // 2) % RING
    z = leaf // (2 * RING)
    first = y + core * (z - y)
    second = z + core * (y - z)

    def device(index):
        index = lax.rem(index + devices, devices)
        return (index // 4, lax.rem(index, 4))

    def chip(a, b):
        a = lax.rem(a + RING, RING)
        b = lax.rem(b + RING, RING)
        row = a + core * (b - a)
        layer = b + core * (a - b)
        return ((layer * RING + row) * 2 + core, sub)

    def across(a, b):
        to_leaf, to_sub = chip(a, b)
        return (to_leaf + 1 - 2 * core, to_sub)

    right, left = chip(first, second + 1), chip(first, second - 1)
    sibling = (leaf + 1 - 2 * core, sub)

    barrier = pltpu.get_barrier_semaphore()
    friends = [device(me + s * k) for k in (1, 2, 4, 8, 16) for s in (1, -1)]
    friends += [right, left]
    friends += [chip(first + k, second) for k in range(1, RING)]
    friends += [across(first + k, second) for k in range(RING)]
    for friend in friends:
        pl.semaphore_signal(barrier, inc=1, device_id=friend, device_id_type=MESH)

    def load(source, target, index):
        copy = pltpu.make_async_copy(source, target, load_sem.at[index])
        copy.start()
        return copy

    light_loads = [
        load(light_hbm.at[:, pl.ds(t * LEAF, LEAF)], window.at[HALO + t], 4 + t) for t in range(LEAVES)
    ]
    basis_load = load(basis_hbm, basis, 1)
    transfer_load = load(transfer_hbm, transfer, 2)
    coupling_load = load(coupling_hbm, coupling, 3)

    geo[HALO : HALO + LEAVES] = jnp.zeros((LEAVES, 8, LEAF), F32)
    for t in range(LEAVES):
        geo[HALO + t, 0:4, :] = probes_ref[:, t * LEAF : (t + 1) * LEAF].astype(F32)
    lanes = lax.broadcasted_iota(jnp.int32, (LIGHTS, 2 * RANK), 1)
    mask[0] = jnp.where(lanes < RANK, 1.0, 0.0).astype(BF16)
    mask[1] = jnp.where(lanes < RANK, 0.0, 1.0).astype(BF16)

    def send(source, target, send_sem, recv_sem, to):
        return pltpu.make_async_remote_copy(
            src_ref=source,
            dst_ref=target,
            send_sem=send_sem,
            recv_sem=recv_sem,
            device_id=to,
            device_id_type=MESH,
        )

    def halo(ref, index):
        down = send(
            ref.at[pl.ds(HALO, HALO)],
            ref.at[pl.ds(HALO + LEAVES, HALO)],
            halo_send.at[index],
            halo_recv.at[index],
            device(me - 1),
        )
        up = send(
            ref.at[pl.ds(LEAVES, HALO)],
            ref.at[pl.ds(0, HALO)],
            halo_send.at[index + 1],
            halo_recv.at[index + 1],
            device(me + 1),
        )
        down.start()
        up.start()
        return [down, up]

    for light_load in light_loads:
        light_load.wait()
    basis_load.wait()

    my_block = (core * LINE + second * RING + first) * PER_CHIP + core * 2
    pairs = []
    for q in range(LEAVES // 2):
        parts = []
        for t in (2 * q, 2 * q + 1):
            parts.append(lax.dot_general(window[HALO + t], basis[t], NT, preferred_element_type=F32))
        pairs.append(jnp.concatenate(parts, axis=1).astype(BF16))
    for i in range(2):
        lower, higher = pairs[i], pairs[2 + i]
        pool[my_block + i] = jnp.where(core == 0, lower.astype(F32), higher.astype(F32)).astype(BF16)
        traded[i] = jnp.where(core == 0, higher.astype(F32), lower.astype(F32)).astype(BF16)
    other_block = ((1 - core) * LINE + first * RING + second) * PER_CHIP + core * 2

    pl.semaphore_wait(barrier, len(friends))

    ours, theirs = pool.at[pl.ds(my_block, 2)], pool.at[pl.ds(other_block, 2)]
    for k in range(RING):
        send(traded, theirs, first_send, first_recv.at[second // 2], across(first, second + k)).start()
        if k:
            send(ours, ours, first_send, first_recv.at[first // 2], chip(first + k, second)).start()
    halos = halo(geo, 0) + halo(window, 2)

    transfer_load.wait()
    stacked = jnp.concatenate(pairs, axis=1)
    level0 = jnp.dot(stacked, transfer[...], preferred_element_type=F32)

    def twice(value):
        return jnp.concatenate([value, value], axis=1)

    def exact(value, matrix, dims=(((1,), (0,)), ((), ()))):
        high = value.astype(BF16)
        rest = value - high.astype(F32)
        middle = rest.astype(BF16)
        low = (rest - middle.astype(F32)).astype(BF16)
        parts = jnp.concatenate([high, middle, low], axis=0)
        product = lax.dot_general(parts, matrix, dims, preferred_element_type=F32)
        return product[:LIGHTS] + (product[LIGHTS : 2 * LIGHTS] + product[2 * LIGHTS :])

    def climb(height, value):
        upward[height] = twice(value)
        stride = 2 ** (height + 1)
        moves = [
            send(
                upward.at[height],
                below.at[height],
                tree_send.at[3 * height],
                tree_recv.at[3 * height],
                device(me + stride),
            ),
            send(
                upward.at[height],
                above.at[height],
                tree_send.at[3 * height + 1],
                tree_recv.at[3 * height + 1],
                device(me - stride),
            ),
        ]
        if height < UPLV:
            parity = (me // 2**height) % 2
            mine[height] = twice(exact(value, up_ref[height, parity]))
            swap = send(
                mine.at[height],
                partner.at[height],
                tree_send.at[3 * height + 2],
                tree_recv.at[3 * height + 2],
                device(me + (1 - 2 * parity) * 2**height),
            )
            swap.start()
            moves.append(swap)
        moves[0].start()
        moves[1].start()
        return moves

    tree = [climb(0, level0)]

    def chunk(n, sign):
        b = lax.rem(second - sign * (n // CHUNKS) + RING, RING)
        q = lax.rem(first // 2 + n + (CHUNKS // 2) * (sign < 0) + 2 * RING, CHUNKS)
        return pool.at[pl.ds((core * LINE + b * RING) * PER_CHIP + q * CHUNK, CHUNK)]

    def arrive(q):
        at = lax.rem(first // 2 + q, CHUNKS)
        ref = pool.at[pl.ds(0, CHUNK if q else CHUNK - 2)]
        send(ref, ref, first_send, first_recv.at[at], sibling).wait_recv()

    def to_right(n):
        ref = chunk(n, 1)
        send(ref, ref, right_send, right_recv.at[n], right).start()

    def to_left(n):
        ref = chunk(n, -1)
        send(ref, ref, left_send, left_recv.at[n], left).start()

    def to_sibling(ref):
        send(ref, ref, sib_send, sib_recv, sibling).start()

    def spread_columns(t):
        turned = jnp.transpose(geo[HALO + t])
        for k in range(4):
            value = turned[:, k : k + 1]
            if k == 3:
                value = value * soften
            columns[t, k] = jnp.broadcast_to(value, (LEAF, 128))

    def add_tile(t, w, shift, before, slot):
        rows = geo[w]
        row_x, row_y, row_z, row_a = (rows[0:1] - shift, rows[1:2], rows[2:3], rows[3:4])
        for i in range(0, LEAF, 32):
            sides = []
            for lane in (0, 128):
                cut = slice(lane, lane + 128)
                dx = columns[t, 0, i : i + 32] - row_x[:, cut]
                dy = columns[t, 1, i : i + 32] - row_y[:, cut]
                dz = columns[t, 2, i : i + 32] - row_z[:, cut]
                total = dx * dx + soften + dy * dy + dz * dz
                guess = pl.reciprocal(total, approx=True)
                guess = guess * (2.0 - total * guess)
                sides.append((columns[t, 3, i : i + 32] * row_a[:, cut] * guess).astype(BF16))
            tile[slot, i : i + 32, :] = jnp.concatenate(sides, axis=1)
        near_terms[t] = before + lax.dot_general(window[w], tile[slot], NT, preferred_element_type=F32)

    def near_pair(p, slot):
        t, k = p // NNEAR, p % NNEAR
        w = (near_list_ref[k, t] - LEAVES * me + HALO) & (LEAVES + 2 * HALO - 1)
        add_tile(t, w, (t + HALO - w).astype(F32) * spacing, near_terms[t], slot)

    def encode(t, carry):
        for c in range(NFAR):
            entry = far_list_ref[t, c]
            layer, row, group = entry >> 9, (entry >> 6) & 7, (entry >> 2) & 1
            low, high = layer * RING + row, row * RING + layer + LINE
            place = low + group * (high - low)
            codes[t, c] = place * 8 + ((entry >> 5) & 1) * 4 + (entry & 3)
        return carry

    for t in range(LEAVES):
        spread_columns(t)
    lax.fori_loop(0, LEAVES, encode, 0)
    for t in range(LEAVES // 2):
        add_tile(t, HALO + t, 0.0, 0.0, t % TILES)


    def rejoin(height):
        tree[height][2].wait_recv()
        total = mine[height] + partner[height]
        tree.append(climb(height + 1, total[:, :RANK]))

    arrive(0)
    to_right(0)
    arrive(2)
    to_left(0)
    arrive(1)
    to_right(1)
    arrive(3)
    to_left(1)
    for n in (2, 3):
        to_right(n)
        to_left(n)
    for n in range(CHUNKS):
        to_sibling(chunk(n, 1))
    rejoin(0)
    for t in range(LEAVES // 2, LEAVES):
        add_tile(t, HALO + t, 0.0, 0.0, t % TILES)
    for move in halos:
        move.wait_recv()

    def take(n, onward):
        ref = chunk(n + CHUNKS, 1)
        send(ref, ref, right_send, right_recv.at[n], right).wait_recv()
        if onward:
            send(ref, ref, right_send, right_recv.at[n + CHUNKS], right).start()
        ref_left = chunk(n + CHUNKS, -1)
        send(ref_left, ref_left, left_send, left_recv.at[n], left).wait_recv()
        if onward:
            send(ref_left, ref_left, left_send, left_recv.at[n + CHUNKS], left).start()
        to_sibling(ref)
        to_sibling(ref_left)

    def couple(height):
        tree[height][0].wait_recv()
        tree[height][1].wait_recv()
        cluster = me // 2**height
        low = jnp.where(cluster >= 2, below[height][:, :RANK], 0.0)
        high = jnp.where(cluster + 2 < devices // 2**height, above[height][:, :RANK], 0.0)
        return exact(low, upper_ref[height, 0]) + exact(high, upper_ref[height, 1])

    coupled = []
    def ring_step(n, carry):
        take(n, True)
        for k in range(TILES):
            near_pair(TILES * n + k, k)
        return carry

    for place in range(5):
        lax.fori_loop(2 * place, 2 * place + 2, ring_step, 0)
        if place in (0, 2):
            rejoin(1 + place // 2)
        if place in (1, 3):
            coupled.append(couple(place // 2))
    for p in range(TILES * 10, LEAVES * NNEAR):
        near_pair(p, p % TILES)
    coupled.append(couple(2))

    def last_step(n, carry):
        take(n, False)
        return carry

    lax.fori_loop(10, 12, last_step, 0)

    coupled.append(couple(UPLV))
    downward = coupled[UPLV]
    for height in range(UPLV - 1, -1, -1):
        downward = coupled[height] + exact(downward, up_ref[height, (me // 2**height) % 2], NT)
    pulled[...] = exact(downward, transfer[...], NT)

    lax.fori_loop(12, STEPS, last_step, 0)

    coupling_load.wait()

    others = pool.at[pl.ds((1 - core) * LINE * PER_CHIP, LINE * PER_CHIP)]
    send(others, others, sib_send, sib_recv, sibling).wait_recv()

    for t in range(LEAVES):
        picked = []
        for c in range(0, NFAR, 2):
            two = []
            for k in range(2):
                code = codes[t, c + k]
                block = pool[code >> 1]
                turned = jnp.concatenate([block[:, RANK:], block[:, :RANK]], axis=1)
                two.append(jnp.where((code & 1) == k, block, turned))
            picked.append(two[0] * mask[0] + two[1] * mask[1])
        far = jnp.dot(jnp.concatenate(picked, axis=1), coupling[t], preferred_element_type=F32)
        leaf_far = (far + pulled[:, t * RANK : (t + 1) * RANK]).astype(BF16)
        back = jnp.dot(leaf_far, basis[t], preferred_element_type=F32)
        out_ref[:, t * LEAF : (t + 1) * LEAF] = (near_terms[t] + back).astype(BF16)

    for move in halos + [m for moves in tree for m in moves]:
        move.wait_send()

    def sent(count, send_sem):
        ref = pool.at[pl.ds(0, count)]
        send(ref, ref, send_sem, sib_recv, sibling).wait_send()

    sent(2 * (2 * RING - 1), first_send)
    sent(STEPS * CHUNK, right_send)
    sent(STEPS * CHUNK, left_send)
    sent(LINE * PER_CHIP, sib_send)


def solution(mesh):
    devices = mesh.shape["leaf"] * mesh.shape["sub"]

    def per_device(
        light,
        probes,
        near_list,
        far_list,
        leaf_basis,
        leaf_transfer,
        far_coupling,
        up_transfer,
        upper_coupling,
    ):
        any_space = pl.BlockSpec(memory_space=pl.ANY)
        vmem = pl.BlockSpec(memory_space=pltpu.VMEM)
        smem = pl.BlockSpec(memory_space=pltpu.SMEM)
        dma = pltpu.SemaphoreType.DMA
        slots = LEAVES + 2 * HALO
        return pl.pallas_call(
            functools.partial(kernel, devices),
            out_shape=pltpu.VMEM((LIGHTS, LEAVES * LEAF), BF16),
            in_specs=[any_space, vmem, smem, smem, any_space, any_space, any_space, vmem, vmem],
            out_specs=vmem,
            scratch_shapes=[
                pltpu.VMEM((slots, LIGHTS, LEAF), BF16),
                pltpu.VMEM((slots, 8, LEAF), F32),
                pltpu.VMEM((LEAVES, 4, LEAF, 128), F32),
                pltpu.VMEM((LEAVES, RANK, LEAF), BF16),
                pltpu.VMEM((LEAVES * RANK, RANK), BF16),
                pltpu.VMEM((LEAVES, NFAR * RANK, RANK), BF16),
                pltpu.VMEM((2 * LINE * PER_CHIP, LIGHTS, 2 * RANK), BF16),
                pltpu.VMEM((2, LIGHTS, 2 * RANK), BF16),
                pltpu.VMEM((LEAVES, LIGHTS, LEAF), F32),
                pltpu.VMEM((LIGHTS, LEAVES * RANK), F32),
                pltpu.VMEM((TILES, LEAF, LEAF), BF16),
                pltpu.VMEM((UPLV + 1, LIGHTS, 2 * RANK), F32),
                pltpu.VMEM((UPLV, LIGHTS, 2 * RANK), F32),
                pltpu.VMEM((UPLV, LIGHTS, 2 * RANK), F32),
                pltpu.VMEM((UPLV + 1, LIGHTS, 2 * RANK), F32),
                pltpu.VMEM((UPLV + 1, LIGHTS, 2 * RANK), F32),
                pltpu.VMEM((2, LIGHTS, 2 * RANK), BF16),
                pltpu.SMEM((LEAVES, NFAR), jnp.int32),
                dma((4 + LEAVES,)),
                dma((4,)),
                dma((4,)),
                dma,
                dma((CHUNKS,)),
                dma,
                dma((STEPS,)),
                dma,
                dma((STEPS,)),
                dma,
                dma,
                dma((3 * (UPLV + 1),)),
                dma((3 * (UPLV + 1),)),
            ],
            compiler_params=pltpu.CompilerParams(
                collective_id=0, has_side_effects=True, vmem_limit_bytes=56 * 2**20
            ),
        )(
            light,
            probes,
            near_list.T,
            far_list,
            jnp.swapaxes(leaf_basis, 1, 2),
            leaf_transfer.reshape(LEAVES * RANK, RANK),
            far_coupling.reshape(LEAVES, NFAR * RANK, RANK),
            up_transfer,
            upper_coupling,
        )

    return jax.shard_map(
        per_device,
        mesh=mesh,
        in_specs=(
            P(None, ("leaf", "sub")),
            P(None, ("leaf", "sub")),
            P(("leaf", "sub"), None),
            P(("leaf", "sub"), None),
            P(("leaf", "sub"), None, None),
            P(("leaf", "sub"), None, None),
            P(("leaf", "sub"), None, None, None),
            P(),
            P(),
        ),
        out_specs=P(None, ("leaf", "sub")),
        check_vma=False,
    )
```

```python
import functools

import jax
import jax.numpy as jnp
from jax import lax
from jax.experimental import pallas as pl
from jax.experimental.pallas import tpu as pltpu
from jax.sharding import PartitionSpec as P

MESH = pl.DeviceIdType.MESH
F32, BF16 = jnp.float32, jnp.bfloat16

HALO = 4
UPLV = 3
LEAF = 256
RANK = 64
LIGHTS = 32
LEAVES = 8
NNEAR = 4
NFAR = 32
soften = 0.0025
spacing = 0.25

RING = 8
LINE = RING * RING
PER_CHIP = 4
CHUNKS = 4
PART = RING // CHUNKS
CHUNK = PART * PER_CHIP
STEPS = RING // 2 * CHUNKS - CHUNKS // 2
SPLIT = CHUNKS // 4
TILES = 3

NT = (((1,), (1,)), ((), ()))


def kernel(
    devices,
    light_hbm,
    probes_ref,
    near_list_ref,
    far_list_ref,
    basis_hbm,
    transfer_hbm,
    coupling_hbm,
    up_ref,
    upper_ref,
    out_ref,
    window,
    geo,
    columns,
    basis,
    transfer,
    coupling,
    pool,
    traded,
    near_terms,
    pulled,
    tile,
    upward,
    mine,
    partner,
    below,
    above,
    mask,
    codes,
    load_sem,
    halo_send,
    halo_recv,
    first_send,
    first_recv,
    right_send,
    right_recv,
    left_send,
    left_recv,
    sib_send,
    sib_recv,
    tree_send,
    tree_recv,
):
    leaf = lax.axis_index("leaf")
    sub = lax.axis_index("sub")
    me = leaf * 4 + sub
    core = leaf % 2
    y = (leaf // 2) % RING
    z = leaf // (2 * RING)
    first = y + core * (z - y)
    second = z + core * (y - z)

    def device(index):
        index = lax.rem(index + devices, devices)
        return (index // 4, lax.rem(index, 4))

    def chip(a, b):
        a = lax.rem(a + RING, RING)
        b = lax.rem(b + RING, RING)
        row = a + core * (b - a)
        layer = b + core * (a - b)
        return ((layer * RING + row) * 2 + core, sub)

    def across(a, b):
        to_leaf, to_sub = chip(a, b)
        return (to_leaf + 1 - 2 * core, to_sub)

    right, left = chip(first, second + 1), chip(first, second - 1)
    sibling = (leaf + 1 - 2 * core, sub)

    barrier = pltpu.get_barrier_semaphore()
    friends = [device(me + s * k) for k in (1, 2, 4, 8, 16) for s in (1, -1)]
    friends += [right, left]
    friends += [chip(first + k, second) for k in range(1, RING)]
    friends += [across(first + k, second) for k in range(RING)]
    for friend in friends:
        pl.semaphore_signal(barrier, inc=1, device_id=friend, device_id_type=MESH)

    def load(source, target, index):
        copy = pltpu.make_async_copy(source, target, load_sem.at[index])
        copy.start()
        return copy

    light_loads = [
        load(light_hbm.at[:, pl.ds(t * LEAF, LEAF)], window.at[HALO + t], 4 + t) for t in range(LEAVES)
    ]
    basis_load = load(basis_hbm, basis, 1)
    transfer_load = load(transfer_hbm, transfer, 2)
    coupling_load = load(coupling_hbm, coupling, 3)

    geo[HALO : HALO + LEAVES] = jnp.zeros((LEAVES, 8, LEAF), F32)
    for t in range(LEAVES):
        geo[HALO + t, 0:4, :] = probes_ref[:, t * LEAF : (t + 1) * LEAF].astype(F32)
    lanes = lax.broadcasted_iota(jnp.int32, (LIGHTS, 2 * RANK), 1)
    mask[0] = jnp.where(lanes < RANK, 1.0, 0.0).astype(BF16)
    mask[1] = jnp.where(lanes < RANK, 0.0, 1.0).astype(BF16)

    def send(source, target, send_sem, recv_sem, to):
        return pltpu.make_async_remote_copy(
            src_ref=source,
            dst_ref=target,
            send_sem=send_sem,
            recv_sem=recv_sem,
            device_id=to,
            device_id_type=MESH,
        )

    def halo(ref, index):
        down = send(
            ref.at[pl.ds(HALO, HALO)],
            ref.at[pl.ds(HALO + LEAVES, HALO)],
            halo_send.at[index],
            halo_recv.at[index],
            device(me - 1),
        )
        up = send(
            ref.at[pl.ds(LEAVES, HALO)],
            ref.at[pl.ds(0, HALO)],
            halo_send.at[index + 1],
            halo_recv.at[index + 1],
            device(me + 1),
        )
        down.start()
        up.start()
        return [down, up]

    for light_load in light_loads:
        light_load.wait()
    basis_load.wait()

    my_block = (core * LINE + second * RING + first) * PER_CHIP + core * 2
    pairs = []
    for q in range(LEAVES // 2):
        parts = []
        for t in (2 * q, 2 * q + 1):
            parts.append(lax.dot_general(window[HALO + t], basis[t], NT, preferred_element_type=F32))
        pairs.append(jnp.concatenate(parts, axis=1).astype(BF16))
    for i in range(2):
        lower, higher = pairs[i], pairs[2 + i]
        pool[my_block + i] = jnp.where(core == 0, lower.astype(F32), higher.astype(F32)).astype(BF16)
        traded[i] = jnp.where(core == 0, higher.astype(F32), lower.astype(F32)).astype(BF16)
    other_block = ((1 - core) * LINE + first * RING + second) * PER_CHIP + core * 2

    pl.semaphore_wait(barrier, len(friends))

    ours, theirs = pool.at[pl.ds(my_block, 2)], pool.at[pl.ds(other_block, 2)]
    for k in (0, 1, -1, 2, -2, 3, -3, 4):
        send(traded, theirs, first_send, first_recv.at[second // PART], across(first, second + k)).start()
        if k:
            send(ours, ours, first_send, first_recv.at[first // PART], chip(first + k, second)).start()
    halos = halo(geo, 0) + halo(window, 2)

    transfer_load.wait()
    stacked = jnp.concatenate(pairs, axis=1)
    level0 = jnp.dot(stacked, transfer[...], preferred_element_type=F32)

    def twice(value):
        return jnp.concatenate([value, value], axis=1)

    def exact(value, matrix, dims=(((1,), (0,)), ((), ()))):
        high = value.astype(BF16)
        rest = value - high.astype(F32)
        middle = rest.astype(BF16)
        low = (rest - middle.astype(F32)).astype(BF16)
        parts = jnp.concatenate([high, middle, low], axis=0)
        product = lax.dot_general(parts, matrix, dims, preferred_element_type=F32)
        return product[:LIGHTS] + (product[LIGHTS : 2 * LIGHTS] + product[2 * LIGHTS :])

    def climb(height, value):
        upward[height] = twice(value)
        stride = 2 ** (height + 1)
        moves = [
            send(
                upward.at[height],
                below.at[height],
                tree_send.at[3 * height],
                tree_recv.at[3 * height],
                device(me + stride),
            ),
            send(
                upward.at[height],
                above.at[height],
                tree_send.at[3 * height + 1],
                tree_recv.at[3 * height + 1],
                device(me - stride),
            ),
        ]
        if height < UPLV:
            parity = (me // 2**height) % 2
            mine[height] = twice(exact(value, up_ref[height, parity]))
            swap = send(
                mine.at[height],
                partner.at[height],
                tree_send.at[3 * height + 2],
                tree_recv.at[3 * height + 2],
                device(me + (1 - 2 * parity) * 2**height),
            )
            swap.start()
            moves.append(swap)
        moves[0].start()
        moves[1].start()
        return moves

    tree = [climb(0, level0)]

    def place_of(n, sign):
        p = lax.rem(n + (CHUNKS // 2) * (sign < 0), CHUNKS)
        return lax.rem(2 * p, CHUNKS) + p // (CHUNKS // 2)

    def chunk(n, sign):
        b = lax.rem(second - sign * (n // CHUNKS) + RING, RING)
        q = lax.rem(first // PART + place_of(n, sign), CHUNKS)
        return pool.at[pl.ds((core * LINE + b * RING) * PER_CHIP + q * CHUNK, CHUNK)]

    def arrive(q):
        at = lax.rem(first // PART + q, CHUNKS)
        ref = pool.at[pl.ds(0, CHUNK if q else CHUNK - 2)]
        send(ref, ref, first_send, first_recv.at[at], sibling).wait_recv()

    def to_right(n):
        ref = chunk(n, 1)
        send(ref, ref, right_send, right_recv.at[n], right).start()

    def to_left(n):
        ref = chunk(n, -1)
        send(ref, ref, left_send, left_recv.at[n], left).start()

    def to_sibling(ref):
        send(ref, ref, sib_send, sib_recv, sibling).start()

    def spread_columns(t):
        turned = jnp.transpose(geo[HALO + t])
        for k in range(4):
            value = turned[:, k : k + 1]
            if k == 3:
                value = value * soften
            columns[t, k] = jnp.broadcast_to(value, (LEAF, 128))

    def add_tile(t, w, shift, before, slot):
        rows = geo[w]
        row_x, row_y, row_z, row_a = (rows[0:1] - shift, rows[1:2], rows[2:3], rows[3:4])
        for i in range(0, LEAF, 32):
            sides = []
            for lane in (0, 128):
                cut = slice(lane, lane + 128)
                dx = columns[t, 0, i : i + 32] - row_x[:, cut]
                dy = columns[t, 1, i : i + 32] - row_y[:, cut]
                dz = columns[t, 2, i : i + 32] - row_z[:, cut]
                total = dx * dx + soften + dy * dy + dz * dz
                guess = pl.reciprocal(total, approx=True)
                guess = guess * (2.0 - total * guess)
                sides.append((columns[t, 3, i : i + 32] * row_a[:, cut] * guess).astype(BF16))
            tile[slot, i : i + 32, :] = jnp.concatenate(sides, axis=1)
        near_terms[t] = before + lax.dot_general(window[w], tile[slot], NT, preferred_element_type=F32)

    def near_pair(p, slot):
        t, k = p // NNEAR, p % NNEAR
        w = (near_list_ref[k, t] - LEAVES * me + HALO) & (LEAVES + 2 * HALO - 1)
        add_tile(t, w, (t + HALO - w).astype(F32) * spacing, near_terms[t], slot)

    def encode(t, carry):
        for c in range(NFAR):
            entry = far_list_ref[t, c]
            layer, row, group = entry >> 9, (entry >> 6) & 7, (entry >> 2) & 1
            low, high = layer * RING + row, row * RING + layer + LINE
            place = low + group * (high - low)
            codes[t, c] = place * 8 + ((entry >> 5) & 1) * 4 + (entry & 3)
        return carry

    for t in range(LEAVES):
        spread_columns(t)
    for t in range(LEAVES // 2):
        add_tile(t, HALO + t, 0.0, 0.0, t % TILES)


    def rejoin(height):
        tree[height][2].wait_recv()
        total = mine[height] + partner[height]
        tree.append(climb(height + 1, total[:, :RANK]))

    for n in range(CHUNKS // 2):
        arrive(2 * n)
        to_right(n)
        arrive(2 * n + 1)
        to_left(n)
    for n in range(CHUNKS // 2, CHUNKS):
        to_right(n)
        to_left(n)
    line = pool.at[pl.ds((core * LINE + second * RING) * PER_CHIP, RING * PER_CHIP)]
    to_sibling(line)
    rejoin(0)
    lax.fori_loop(0, LEAVES, encode, 0)
    for t in range(LEAVES // 2, LEAVES):
        add_tile(t, HALO + t, 0.0, 0.0, t % TILES)
    for move in halos:
        move.wait_recv()

    def take(n, onward):
        ref = chunk(n + CHUNKS, 1)
        send(ref, ref, right_send, right_recv.at[n], right).wait_recv()
        if onward:
            send(ref, ref, right_send, right_recv.at[n + CHUNKS], right).start()
        ref_left = chunk(n + CHUNKS, -1)
        send(ref_left, ref_left, left_send, left_recv.at[n], left).wait_recv()
        if onward:
            send(ref_left, ref_left, left_send, left_recv.at[n + CHUNKS], left).start()
        to_sibling(ref)
        to_sibling(ref_left)

    def couple(height):
        tree[height][0].wait_recv()
        tree[height][1].wait_recv()
        cluster = me // 2**height
        low = jnp.where(cluster >= 2, below[height][:, :RANK], 0.0)
        high = jnp.where(cluster + 2 < devices // 2**height, above[height][:, :RANK], 0.0)
        return exact(low, upper_ref[height, 0]) + exact(high, upper_ref[height, 1])

    coupled = []
    def ring_step(n, carry):
        for k in range(SPLIT):
            take(SPLIT * n + k, True)
        for k in range(TILES):
            near_pair(TILES * n + k, k)
        return carry

    for place in range(5):
        for n in (2 * place, 2 * place + 1):
            ring_step(n, 0)
        if place in (0, 2):
            rejoin(1 + place // 2)
        if place in (1, 3):
            coupled.append(couple(place // 2))
    for p in range(TILES * 10, LEAVES * NNEAR):
        near_pair(p, p % TILES)
    coupled.append(couple(2))

    def last_step(n, carry):
        take(n, False)
        return carry

    for n in range(10 * SPLIT, 12 * SPLIT):
        last_step(n, 0)

    coupled.append(couple(UPLV))
    downward = coupled[UPLV]
    for height in range(UPLV - 1, -1, -1):
        downward = coupled[height] + exact(downward, up_ref[height, (me // 2**height) % 2], NT)
    pulled[...] = exact(downward, transfer[...], NT)

    for n in range(12 * SPLIT, STEPS):
        last_step(n, 0)

    coupling_load.wait()

    for move in halos + [m for moves in tree for m in moves]:
        move.wait_send()

    def sent(count, send_sem):
        ref = pool.at[pl.ds(0, count)]
        send(ref, ref, send_sem, sib_recv, sibling).wait_send()

    sent(2 * (2 * RING - 1), first_send)
    sent(STEPS * CHUNK, right_send)
    sent(STEPS * CHUNK, left_send)

    others = pool.at[pl.ds((1 - core) * LINE * PER_CHIP, LINE * PER_CHIP)]
    send(others, others, sib_send, sib_recv, sibling).wait_recv()

    for t in range(LEAVES):
        picked = []
        for c in range(0, NFAR, 2):
            two = []
            for k in range(2):
                code = codes[t, c + k]
                block = pool[code >> 1]
                turned = jnp.concatenate([block[:, RANK:], block[:, :RANK]], axis=1)
                two.append(jnp.where((code & 1) == k, block, turned))
            picked.append(two[0] * mask[0] + two[1] * mask[1])
        far = jnp.dot(jnp.concatenate(picked, axis=1), coupling[t], preferred_element_type=F32)
        leaf_far = (far + pulled[:, t * RANK : (t + 1) * RANK]).astype(BF16)
        back = jnp.dot(leaf_far, basis[t], preferred_element_type=F32)
        out_ref[:, t * LEAF : (t + 1) * LEAF] = (near_terms[t] + back).astype(BF16)

    sent(LINE * PER_CHIP, sib_send)


def solution(mesh):
    devices = mesh.shape["leaf"] * mesh.shape["sub"]

    def per_device(
        light,
        probes,
        near_list,
        far_list,
        leaf_basis,
        leaf_transfer,
        far_coupling,
        up_transfer,
        upper_coupling,
    ):
        any_space = pl.BlockSpec(memory_space=pl.ANY)
        vmem = pl.BlockSpec(memory_space=pltpu.VMEM)
        smem = pl.BlockSpec(memory_space=pltpu.SMEM)
        dma = pltpu.SemaphoreType.DMA
        slots = LEAVES + 2 * HALO
        return pl.pallas_call(
            functools.partial(kernel, devices),
            out_shape=pltpu.VMEM((LIGHTS, LEAVES * LEAF), BF16),
            in_specs=[any_space, vmem, smem, smem, any_space, any_space, any_space, vmem, vmem],
            out_specs=vmem,
            scratch_shapes=[
                pltpu.VMEM((slots, LIGHTS, LEAF), BF16),
                pltpu.VMEM((slots, 8, LEAF), F32),
                pltpu.VMEM((LEAVES, 4, LEAF, 128), F32),
                pltpu.VMEM((LEAVES, RANK, LEAF), BF16),
                pltpu.VMEM((LEAVES * RANK, RANK), BF16),
                pltpu.VMEM((LEAVES, NFAR * RANK, RANK), BF16),
                pltpu.VMEM((2 * LINE * PER_CHIP, LIGHTS, 2 * RANK), BF16),
                pltpu.VMEM((2, LIGHTS, 2 * RANK), BF16),
                pltpu.VMEM((LEAVES, LIGHTS, LEAF), F32),
                pltpu.VMEM((LIGHTS, LEAVES * RANK), F32),
                pltpu.VMEM((TILES, LEAF, LEAF), BF16),
                pltpu.VMEM((UPLV + 1, LIGHTS, 2 * RANK), F32),
                pltpu.VMEM((UPLV, LIGHTS, 2 * RANK), F32),
                pltpu.VMEM((UPLV, LIGHTS, 2 * RANK), F32),
                pltpu.VMEM((UPLV + 1, LIGHTS, 2 * RANK), F32),
                pltpu.VMEM((UPLV + 1, LIGHTS, 2 * RANK), F32),
                pltpu.VMEM((2, LIGHTS, 2 * RANK), BF16),
                pltpu.SMEM((LEAVES, NFAR), jnp.int32),
                dma((4 + LEAVES,)),
                dma((4,)),
                dma((4,)),
                dma,
                dma((CHUNKS,)),
                dma,
                dma((STEPS,)),
                dma,
                dma((STEPS,)),
                dma,
                dma,
                dma((3 * (UPLV + 1),)),
                dma((3 * (UPLV + 1),)),
            ],
            compiler_params=pltpu.CompilerParams(
                collective_id=0, has_side_effects=True, vmem_limit_bytes=56 * 2**20
            ),
        )(
            light,
            probes,
            near_list.T,
            far_list,
            jnp.swapaxes(leaf_basis, 1, 2),
            leaf_transfer.reshape(LEAVES * RANK, RANK),
            far_coupling.reshape(LEAVES, NFAR * RANK, RANK),
            up_transfer,
            upper_coupling,
        )

    return jax.shard_map(
        per_device,
        mesh=mesh,
        in_specs=(
            P(None, ("leaf", "sub")),
            P(None, ("leaf", "sub")),
            P(("leaf", "sub"), None),
            P(("leaf", "sub"), None),
            P(("leaf", "sub"), None, None),
            P(("leaf", "sub"), None, None),
            P(("leaf", "sub"), None, None, None),
            P(),
            P(),
        ),
        out_specs=P(None, ("leaf", "sub")),
        check_vma=False,
    )
```

```python
import functools

import jax
import jax.numpy as jnp
from jax import lax
from jax.experimental import pallas as pl
from jax.experimental.pallas import tpu as pltpu
from jax.sharding import PartitionSpec as P

MESH = pl.DeviceIdType.MESH
F32, BF16 = jnp.float32, jnp.bfloat16

HALO = 4
UPLV = 3
LEAF = 256
RANK = 64
LIGHTS = 32
LEAVES = 8
NNEAR = 4
NFAR = 32
soften = 0.0025
spacing = 0.25

RING = 8
LINE = RING * RING
PER_CHIP = 4
CHUNKS = 4
PART = RING // CHUNKS
CHUNK = PART * PER_CHIP
STEPS = RING // 2 * CHUNKS - CHUNKS // 2
SPLIT = CHUNKS // 4
TILES = 3

NT = (((1,), (1,)), ((), ()))


def kernel(
    devices,
    light_hbm,
    probes_hbm,
    near_list_hbm,
    far_list_hbm,
    basis_hbm,
    transfer_hbm,
    coupling_hbm,
    up_hbm,
    upper_hbm,
    out_ref,
    near_list_ref,
    far_list_ref,
    probes_ref,
    up_ref,
    upper_ref,
    window,
    geo,
    columns,
    basis,
    transfer,
    coupling,
    pool,
    traded,
    near_terms,
    pulled,
    tile,
    upward,
    mine,
    partner,
    below,
    above,
    mask,
    codes,
    load_sem,
    halo_send,
    halo_recv,
    first_send,
    first_recv,
    right_send,
    right_recv,
    left_send,
    left_recv,
    sib_send,
    sib_recv,
    tree_send,
    tree_recv,
):
    leaf = lax.axis_index("leaf")
    sub = lax.axis_index("sub")
    me = leaf * 4 + sub
    core = leaf % 2
    y = (leaf // 2) % RING
    z = leaf // (2 * RING)
    first = y + core * (z - y)
    second = z + core * (y - z)

    def device(index):
        index = lax.rem(index + devices, devices)
        return (index // 4, lax.rem(index, 4))

    def chip(a, b):
        a = lax.rem(a + RING, RING)
        b = lax.rem(b + RING, RING)
        row = a + core * (b - a)
        layer = b + core * (a - b)
        return ((layer * RING + row) * 2 + core, sub)

    def across(a, b):
        to_leaf, to_sub = chip(a, b)
        return (to_leaf + 1 - 2 * core, to_sub)

    right, left = chip(first, second + 1), chip(first, second - 1)
    sibling = (leaf + 1 - 2 * core, sub)

    barrier = pltpu.get_barrier_semaphore()
    friends = [device(me + s * k) for k in (1, 2, 4, 8, 16) for s in (1, -1)]
    friends += [right, left]
    friends += [chip(first + k, second) for k in range(1, RING)]
    friends += [across(first + k, second) for k in range(RING)]
    for friend in friends:
        pl.semaphore_signal(barrier, inc=1, device_id=friend, device_id_type=MESH)

    def load(source, target, index):
        copy = pltpu.make_async_copy(source, target, load_sem.at[index])
        copy.start()
        return copy

    probes_load = load(probes_hbm, probes_ref, 0)
    light_loads = [
        load(light_hbm.at[:, pl.ds(t * LEAF, LEAF)], window.at[HALO + t], 4 + t) for t in range(LEAVES)
    ]
    basis_load = load(basis_hbm, basis, 1)
    transfer_load = load(transfer_hbm, transfer, 2)
    coupling_load = load(coupling_hbm, coupling, 3)
    near_load = load(near_list_hbm, near_list_ref, 6 + LEAVES)
    far_load = load(far_list_hbm, far_list_ref, 7 + LEAVES)
    up_load = load(up_hbm, up_ref, 4 + LEAVES)
    upper_load = load(upper_hbm, upper_ref, 5 + LEAVES)

    probes_load.wait()
    geo[HALO : HALO + LEAVES] = jnp.zeros((LEAVES, 8, LEAF), F32)
    for t in range(LEAVES):
        geo[HALO + t, 0:4, :] = probes_ref[:, t * LEAF : (t + 1) * LEAF].astype(F32)
    lanes = lax.broadcasted_iota(jnp.int32, (LIGHTS, 2 * RANK), 1)
    mask[0] = jnp.where(lanes < RANK, 1.0, 0.0).astype(BF16)
    mask[1] = jnp.where(lanes < RANK, 0.0, 1.0).astype(BF16)

    def send(source, target, send_sem, recv_sem, to):
        return pltpu.make_async_remote_copy(
            src_ref=source,
            dst_ref=target,
            send_sem=send_sem,
            recv_sem=recv_sem,
            device_id=to,
            device_id_type=MESH,
        )

    def halo(ref, index):
        down = send(
            ref.at[pl.ds(HALO, HALO)],
            ref.at[pl.ds(HALO + LEAVES, HALO)],
            halo_send.at[index],
            halo_recv.at[index],
            device(me - 1),
        )
        up = send(
            ref.at[pl.ds(LEAVES, HALO)],
            ref.at[pl.ds(0, HALO)],
            halo_send.at[index + 1],
            halo_recv.at[index + 1],
            device(me + 1),
        )
        down.start()
        up.start()
        return [down, up]

    for light_load in light_loads:
        light_load.wait()
    basis_load.wait()

    my_block = (core * LINE + second * RING + first) * PER_CHIP + core * 2
    pairs = []
    for q in range(LEAVES // 2):
        parts = []
        for t in (2 * q, 2 * q + 1):
            parts.append(lax.dot_general(window[HALO + t], basis[t], NT, preferred_element_type=F32))
        pairs.append(jnp.concatenate(parts, axis=1).astype(BF16))
    for i in range(2):
        lower, higher = pairs[i], pairs[2 + i]
        pool[my_block + i] = jnp.where(core == 0, lower.astype(F32), higher.astype(F32)).astype(BF16)
        traded[i] = jnp.where(core == 0, higher.astype(F32), lower.astype(F32)).astype(BF16)
    other_block = ((1 - core) * LINE + first * RING + second) * PER_CHIP + core * 2

    pl.semaphore_wait(barrier, len(friends))

    ours, theirs = pool.at[pl.ds(my_block, 2)], pool.at[pl.ds(other_block, 2)]
    for k in (0, 1, -1, 2, -2, 3, -3, 4):
        send(traded, theirs, first_send, first_recv.at[second // PART], across(first, second + k)).start()
        if k:
            send(ours, ours, first_send, first_recv.at[first // PART], chip(first + k, second)).start()
    halos = halo(geo, 0) + halo(window, 2)

    transfer_load.wait()
    near_load.wait()
    far_load.wait()
    up_load.wait()
    upper_load.wait()
    stacked = jnp.concatenate(pairs, axis=1)
    level0 = jnp.dot(stacked, transfer[...], preferred_element_type=F32)

    def twice(value):
        return jnp.concatenate([value, value], axis=1)

    def exact(value, matrix, dims=(((1,), (0,)), ((), ()))):
        high = value.astype(BF16)
        rest = value - high.astype(F32)
        middle = rest.astype(BF16)
        low = (rest - middle.astype(F32)).astype(BF16)
        parts = jnp.concatenate([high, middle, low], axis=0)
        product = lax.dot_general(parts, matrix, dims, preferred_element_type=F32)
        return product[:LIGHTS] + (product[LIGHTS : 2 * LIGHTS] + product[2 * LIGHTS :])

    def climb(height, value):
        upward[height] = twice(value)
        stride = 2 ** (height + 1)
        moves = [
            send(
                upward.at[height],
                below.at[height],
                tree_send.at[3 * height],
                tree_recv.at[3 * height],
                device(me + stride),
            ),
            send(
                upward.at[height],
                above.at[height],
                tree_send.at[3 * height + 1],
                tree_recv.at[3 * height + 1],
                device(me - stride),
            ),
        ]
        if height < UPLV:
            parity = (me // 2**height) % 2
            mine[height] = twice(exact(value, up_ref[height, parity]))
            swap = send(
                mine.at[height],
                partner.at[height],
                tree_send.at[3 * height + 2],
                tree_recv.at[3 * height + 2],
                device(me + (1 - 2 * parity) * 2**height),
            )
            swap.start()
            moves.append(swap)
        moves[0].start()
        moves[1].start()
        return moves

    tree = [climb(0, level0)]

    def place_of(n, sign):
        p = lax.rem(n + (CHUNKS // 2) * (sign < 0), CHUNKS)
        return lax.rem(2 * p, CHUNKS) + p // (CHUNKS // 2)

    def chunk(n, sign):
        b = lax.rem(second - sign * (n // CHUNKS) + RING, RING)
        q = lax.rem(first // PART + place_of(n, sign), CHUNKS)
        return pool.at[pl.ds((core * LINE + b * RING) * PER_CHIP + q * CHUNK, CHUNK)]

    def arrive(q):
        at = lax.rem(first // PART + q, CHUNKS)
        ref = pool.at[pl.ds(0, CHUNK if q else CHUNK - 2)]
        send(ref, ref, first_send, first_recv.at[at], sibling).wait_recv()

    def to_right(n):
        ref = chunk(n, 1)
        send(ref, ref, right_send, right_recv.at[n], right).start()

    def to_left(n):
        ref = chunk(n, -1)
        send(ref, ref, left_send, left_recv.at[n], left).start()

    def to_sibling(ref):
        send(ref, ref, sib_send, sib_recv, sibling).start()

    def spread_columns(t):
        turned = jnp.transpose(geo[HALO + t])
        for k in range(4):
            value = turned[:, k : k + 1]
            if k == 3:
                value = value * soften
            columns[t, k] = jnp.broadcast_to(value, (LEAF, 128))

    def add_tile(t, w, shift, before, slot):
        rows = geo[w]
        row_x, row_y, row_z, row_a = (rows[0:1] - shift, rows[1:2], rows[2:3], rows[3:4])
        for i in range(0, LEAF, 32):
            sides = []
            for lane in (0, 128):
                cut = slice(lane, lane + 128)
                dx = columns[t, 0, i : i + 32] - row_x[:, cut]
                dy = columns[t, 1, i : i + 32] - row_y[:, cut]
                dz = columns[t, 2, i : i + 32] - row_z[:, cut]
                total = dx * dx + soften + dy * dy + dz * dz
                guess = pl.reciprocal(total, approx=True)
                guess = guess * (2.0 - total * guess)
                sides.append((columns[t, 3, i : i + 32] * row_a[:, cut] * guess).astype(BF16))
            tile[slot, i : i + 32, :] = jnp.concatenate(sides, axis=1)
        near_terms[t] = before + lax.dot_general(window[w], tile[slot], NT, preferred_element_type=F32)

    def near_pair(p, slot):
        t, k = p // NNEAR, p % NNEAR
        w = (near_list_ref[k, t] - LEAVES * me + HALO) & (LEAVES + 2 * HALO - 1)
        add_tile(t, w, (t + HALO - w).astype(F32) * spacing, near_terms[t], slot)

    def encode(t, carry):
        for c in range(NFAR):
            entry = far_list_ref[t, c]
            layer, row, group = entry >> 9, (entry >> 6) & 7, (entry >> 2) & 1
            low, high = layer * RING + row, row * RING + layer + LINE
            place = low + group * (high - low)
            codes[t, c] = place * 8 + ((entry >> 5) & 1) * 4 + (entry & 3)
        return carry

    for t in range(LEAVES):
        spread_columns(t)
    for t in range(LEAVES // 2):
        add_tile(t, HALO + t, 0.0, 0.0, t % TILES)


    def rejoin(height):
        tree[height][2].wait_recv()
        total = mine[height] + partner[height]
        tree.append(climb(height + 1, total[:, :RANK]))

    for n in range(CHUNKS // 2):
        arrive(2 * n)
        to_right(n)
        arrive(2 * n + 1)
        to_left(n)
    for n in range(CHUNKS // 2, CHUNKS):
        to_right(n)
        to_left(n)
    line = pool.at[pl.ds((core * LINE + second * RING) * PER_CHIP, RING * PER_CHIP)]
    to_sibling(line)
    rejoin(0)
    lax.fori_loop(0, LEAVES, encode, 0)
    for t in range(LEAVES // 2, LEAVES):
        add_tile(t, HALO + t, 0.0, 0.0, t % TILES)
    for move in halos:
        move.wait_recv()

    def take(n, onward):
        ref = chunk(n + CHUNKS, 1)
        send(ref, ref, right_send, right_recv.at[n], right).wait_recv()
        if onward:
            send(ref, ref, right_send, right_recv.at[n + CHUNKS], right).start()
        ref_left = chunk(n + CHUNKS, -1)
        send(ref_left, ref_left, left_send, left_recv.at[n], left).wait_recv()
        if onward:
            send(ref_left, ref_left, left_send, left_recv.at[n + CHUNKS], left).start()
        to_sibling(ref)
        to_sibling(ref_left)

    def couple(height):
        tree[height][0].wait_recv()
        tree[height][1].wait_recv()
        cluster = me // 2**height
        low = jnp.where(cluster >= 2, below[height][:, :RANK], 0.0)
        high = jnp.where(cluster + 2 < devices // 2**height, above[height][:, :RANK], 0.0)
        return exact(low, upper_ref[height, 0]) + exact(high, upper_ref[height, 1])

    coupled = []
    def ring_step(n, carry):
        for k in range(SPLIT):
            take(SPLIT * n + k, True)
        for k in range(TILES):
            near_pair(TILES * n + k, k)
        return carry

    for place in range(5):
        for n in (2 * place, 2 * place + 1):
            ring_step(n, 0)
        if place in (0, 2):
            rejoin(1 + place // 2)
        if place in (1, 3):
            coupled.append(couple(place // 2))
    for p in range(TILES * 10, LEAVES * NNEAR):
        near_pair(p, p % TILES)
    coupled.append(couple(2))

    def last_step(n, carry):
        take(n, False)
        return carry

    for n in range(10 * SPLIT, 12 * SPLIT):
        last_step(n, 0)

    coupled.append(couple(UPLV))
    downward = coupled[UPLV]
    for height in range(UPLV - 1, -1, -1):
        downward = coupled[height] + exact(downward, up_ref[height, (me // 2**height) % 2], NT)
    pulled[...] = exact(downward, transfer[...], NT)

    for n in range(12 * SPLIT, STEPS):
        last_step(n, 0)

    coupling_load.wait()

    for move in halos + [m for moves in tree for m in moves]:
        move.wait_send()

    def sent(count, send_sem):
        ref = pool.at[pl.ds(0, count)]
        send(ref, ref, send_sem, sib_recv, sibling).wait_send()

    sent(2 * (2 * RING - 1), first_send)
    sent(STEPS * CHUNK, right_send)
    sent(STEPS * CHUNK, left_send)

    others = pool.at[pl.ds((1 - core) * LINE * PER_CHIP, LINE * PER_CHIP)]
    send(others, others, sib_send, sib_recv, sibling).wait_recv()

    for t in range(LEAVES):
        picked = []
        for c in range(0, NFAR, 2):
            two = []
            for k in range(2):
                code = codes[t, c + k]
                block = pool[code >> 1]
                turned = jnp.concatenate([block[:, RANK:], block[:, :RANK]], axis=1)
                two.append(jnp.where((code & 1) == k, block, turned))
            picked.append(two[0] * mask[0] + two[1] * mask[1])
        far = jnp.dot(jnp.concatenate(picked, axis=1), coupling[t], preferred_element_type=F32)
        leaf_far = (far + pulled[:, t * RANK : (t + 1) * RANK]).astype(BF16)
        back = jnp.dot(leaf_far, basis[t], preferred_element_type=F32)
        out_ref[:, t * LEAF : (t + 1) * LEAF] = (near_terms[t] + back).astype(BF16)

    sent(LINE * PER_CHIP, sib_send)


def solution(mesh):
    devices = mesh.shape["leaf"] * mesh.shape["sub"]

    def per_device(
        light,
        probes,
        near_list,
        far_list,
        leaf_basis,
        leaf_transfer,
        far_coupling,
        up_transfer,
        upper_coupling,
    ):
        any_space = pl.BlockSpec(memory_space=pl.ANY)
        vmem = pl.BlockSpec(memory_space=pltpu.VMEM)
        dma = pltpu.SemaphoreType.DMA
        slots = LEAVES + 2 * HALO
        return pl.pallas_call(
            functools.partial(kernel, devices),
            out_shape=pltpu.VMEM((LIGHTS, LEAVES * LEAF), BF16),
            in_specs=[any_space] * 9,
            out_specs=vmem,
            scratch_shapes=[
                pltpu.SMEM((NNEAR, LEAVES), jnp.int32),
                pltpu.SMEM((LEAVES, NFAR), jnp.int32),
                pltpu.VMEM((4, LEAVES * LEAF), BF16),
                pltpu.VMEM(up_transfer.shape, BF16),
                pltpu.VMEM(upper_coupling.shape, BF16),
                pltpu.VMEM((slots, LIGHTS, LEAF), BF16),
                pltpu.VMEM((slots, 8, LEAF), F32),
                pltpu.VMEM((LEAVES, 4, LEAF, 128), F32),
                pltpu.VMEM((LEAVES, RANK, LEAF), BF16),
                pltpu.VMEM((LEAVES * RANK, RANK), BF16),
                pltpu.VMEM((LEAVES, NFAR * RANK, RANK), BF16),
                pltpu.VMEM((2 * LINE * PER_CHIP, LIGHTS, 2 * RANK), BF16),
                pltpu.VMEM((2, LIGHTS, 2 * RANK), BF16),
                pltpu.VMEM((LEAVES, LIGHTS, LEAF), F32),
                pltpu.VMEM((LIGHTS, LEAVES * RANK), F32),
                pltpu.VMEM((TILES, LEAF, LEAF), BF16),
                pltpu.VMEM((UPLV + 1, LIGHTS, 2 * RANK), F32),
                pltpu.VMEM((UPLV, LIGHTS, 2 * RANK), F32),
                pltpu.VMEM((UPLV, LIGHTS, 2 * RANK), F32),
                pltpu.VMEM((UPLV + 1, LIGHTS, 2 * RANK), F32),
                pltpu.VMEM((UPLV + 1, LIGHTS, 2 * RANK), F32),
                pltpu.VMEM((2, LIGHTS, 2 * RANK), BF16),
                pltpu.SMEM((LEAVES, NFAR), jnp.int32),
                dma((8 + LEAVES,)),
                dma((4,)),
                dma((4,)),
                dma,
                dma((CHUNKS,)),
                dma,
                dma((STEPS,)),
                dma,
                dma((STEPS,)),
                dma,
                dma,
                dma((3 * (UPLV + 1),)),
                dma((3 * (UPLV + 1),)),
            ],
            compiler_params=pltpu.CompilerParams(
                collective_id=0, has_side_effects=True, vmem_limit_bytes=56 * 2**20
            ),
        )(
            light,
            probes,
            near_list.T,
            far_list,
            jnp.swapaxes(leaf_basis, 1, 2),
            leaf_transfer.reshape(LEAVES * RANK, RANK),
            far_coupling.reshape(LEAVES, NFAR * RANK, RANK),
            up_transfer,
            upper_coupling,
        )

    return jax.shard_map(
        per_device,
        mesh=mesh,
        in_specs=(
            P(None, ("leaf", "sub")),
            P(None, ("leaf", "sub")),
            P(("leaf", "sub"), None),
            P(("leaf", "sub"), None),
            P(("leaf", "sub"), None, None),
            P(("leaf", "sub"), None, None),
            P(("leaf", "sub"), None, None, None),
            P(),
            P(),
        ),
        out_specs=P(None, ("leaf", "sub")),
        check_vma=False,
    )
```

```python
import functools

import jax
import jax.numpy as jnp
from jax import lax
from jax.experimental import pallas as pl
from jax.experimental.pallas import tpu as pltpu
from jax.sharding import PartitionSpec as P

MESH = pl.DeviceIdType.MESH
F32, BF16 = jnp.float32, jnp.bfloat16

HALO = 4
UPLV = 3
LEAF = 256
RANK = 64
LIGHTS = 32
LEAVES = 8
NNEAR = 4
NFAR = 32
soften = 0.0025
spacing = 0.25

RING = 8
LINE = RING * RING
PER_CHIP = 4
CHUNKS = 4
PART = RING // CHUNKS
CHUNK = PART * PER_CHIP
STEPS = RING // 2 * CHUNKS - CHUNKS // 2
SPLIT = CHUNKS // 4
TILES = 3

NT = (((1,), (1,)), ((), ()))


def kernel(
    devices,
    light_hbm,
    probes_hbm,
    near_list_hbm,
    far_list_hbm,
    basis_hbm,
    transfer_hbm,
    coupling_hbm,
    up_hbm,
    upper_hbm,
    out_ref,
    near_list_ref,
    far_list_ref,
    probes_ref,
    up_ref,
    upper_ref,
    window,
    geo,
    columns,
    basis,
    transfer,
    coupling,
    pool,
    traded,
    near_terms,
    pulled,
    tile,
    upward,
    mine,
    partner,
    below,
    above,
    mask,
    codes,
    load_sem,
    halo_send,
    halo_recv,
    first_send,
    first_recv,
    right_send,
    right_recv,
    left_send,
    left_recv,
    sib_send,
    sib_recv,
    tree_send,
    tree_recv,
):
    leaf = lax.axis_index("leaf")
    sub = lax.axis_index("sub")
    me = leaf * 4 + sub
    core = leaf % 2
    y = (leaf // 2) % RING
    z = leaf // (2 * RING)
    first = y + core * (z - y)
    second = z + core * (y - z)

    def device(index):
        index = lax.rem(index + devices, devices)
        return (index // 4, lax.rem(index, 4))

    def chip(a, b):
        a = lax.rem(a + RING, RING)
        b = lax.rem(b + RING, RING)
        row = a + core * (b - a)
        layer = b + core * (a - b)
        return ((layer * RING + row) * 2 + core, sub)

    def across(a, b):
        to_leaf, to_sub = chip(a, b)
        return (to_leaf + 1 - 2 * core, to_sub)

    right, left = chip(first, second + 1), chip(first, second - 1)
    sibling = (leaf + 1 - 2 * core, sub)

    barrier = pltpu.get_barrier_semaphore()
    friends = [device(me + s * k) for k in (1, 2, 4, 8, 16) for s in (1, -1)]
    friends += [right, left]
    friends += [chip(first + k, second) for k in range(1, RING)]
    friends += [across(first + k, second) for k in range(RING)]
    for friend in friends:
        pl.semaphore_signal(barrier, inc=1, device_id=friend, device_id_type=MESH)

    def load(source, target, index):
        copy = pltpu.make_async_copy(source, target, load_sem.at[index])
        copy.start()
        return copy

    probes_load = load(probes_hbm, probes_ref, 0)
    light_loads = [
        load(light_hbm.at[:, pl.ds(t * LEAF, LEAF)], window.at[HALO + t], 4 + t) for t in range(LEAVES)
    ]
    basis_load = load(basis_hbm, basis, 1)
    transfer_load = load(transfer_hbm, transfer, 2)
    coupling_load = load(coupling_hbm, coupling, 3)
    near_load = load(near_list_hbm, near_list_ref, 6 + LEAVES)
    far_load = load(far_list_hbm, far_list_ref, 7 + LEAVES)
    up_load = load(up_hbm, up_ref, 4 + LEAVES)
    upper_load = load(upper_hbm, upper_ref, 5 + LEAVES)

    probes_load.wait()
    geo[HALO : HALO + LEAVES] = jnp.zeros((LEAVES, 8, LEAF), F32)
    for t in range(LEAVES):
        geo[HALO + t, 0:4, :] = probes_ref[:, t * LEAF : (t + 1) * LEAF].astype(F32)
    lanes = lax.broadcasted_iota(jnp.int32, (LIGHTS, 2 * RANK), 1)
    mask[0] = jnp.where(lanes < RANK, 1.0, 0.0).astype(BF16)
    mask[1] = jnp.where(lanes < RANK, 0.0, 1.0).astype(BF16)

    def send(source, target, send_sem, recv_sem, to):
        return pltpu.make_async_remote_copy(
            src_ref=source,
            dst_ref=target,
            send_sem=send_sem,
            recv_sem=recv_sem,
            device_id=to,
            device_id_type=MESH,
        )

    def halo(ref, index):
        down = send(
            ref.at[pl.ds(HALO, HALO)],
            ref.at[pl.ds(HALO + LEAVES, HALO)],
            halo_send.at[index],
            halo_recv.at[index],
            device(me - 1),
        )
        up = send(
            ref.at[pl.ds(LEAVES, HALO)],
            ref.at[pl.ds(0, HALO)],
            halo_send.at[index + 1],
            halo_recv.at[index + 1],
            device(me + 1),
        )
        down.start()
        up.start()
        return [down, up]

    for light_load in light_loads:
        light_load.wait()
    basis_load.wait()

    my_block = (core * LINE + second * RING + first) * PER_CHIP + core * 2
    pairs = []
    for q in range(LEAVES // 2):
        parts = []
        for t in (2 * q, 2 * q + 1):
            parts.append(lax.dot_general(window[HALO + t], basis[t], NT, preferred_element_type=F32))
        pairs.append(jnp.concatenate(parts, axis=1).astype(BF16))
    for i in range(2):
        lower, higher = pairs[i], pairs[2 + i]
        pool[my_block + i] = jnp.where(core == 0, lower.astype(F32), higher.astype(F32)).astype(BF16)
        traded[i] = jnp.where(core == 0, higher.astype(F32), lower.astype(F32)).astype(BF16)
    other_block = ((1 - core) * LINE + first * RING + second) * PER_CHIP + core * 2

    pl.semaphore_wait(barrier, len(friends))

    ours, theirs = pool.at[pl.ds(my_block, 2)], pool.at[pl.ds(other_block, 2)]
    for k in (0, 1, -1, 2, -2, 3, -3, 4):
        send(traded, theirs, first_send, first_recv.at[second // PART], across(first, second + k)).start()
        if k:
            send(ours, ours, first_send, first_recv.at[first // PART], chip(first + k, second)).start()
    halos = halo(geo, 0) + halo(window, 2)

    transfer_load.wait()
    near_load.wait()
    far_load.wait()
    up_load.wait()
    upper_load.wait()
    stacked = jnp.concatenate(pairs, axis=1)
    level0 = jnp.dot(stacked, transfer[...], preferred_element_type=F32)

    def twice(value):
        return jnp.concatenate([value, value], axis=1)

    def exact(value, matrix, dims=(((1,), (0,)), ((), ()))):
        high = value.astype(BF16)
        rest = value - high.astype(F32)
        middle = rest.astype(BF16)
        low = (rest - middle.astype(F32)).astype(BF16)
        parts = jnp.concatenate([high, middle, low], axis=0)
        product = lax.dot_general(parts, matrix, dims, preferred_element_type=F32)
        return product[:LIGHTS] + (product[LIGHTS : 2 * LIGHTS] + product[2 * LIGHTS :])

    def climb(height, value):
        upward[height] = twice(value)
        stride = 2 ** (height + 1)
        moves = [
            send(
                upward.at[height],
                below.at[height],
                tree_send.at[3 * height],
                tree_recv.at[3 * height],
                device(me + stride),
            ),
            send(
                upward.at[height],
                above.at[height],
                tree_send.at[3 * height + 1],
                tree_recv.at[3 * height + 1],
                device(me - stride),
            ),
        ]
        if height < UPLV:
            parity = (me // 2**height) % 2
            mine[height] = twice(exact(value, up_ref[height, parity]))
            swap = send(
                mine.at[height],
                partner.at[height],
                tree_send.at[3 * height + 2],
                tree_recv.at[3 * height + 2],
                device(me + (1 - 2 * parity) * 2**height),
            )
            swap.start()
            moves.append(swap)
        moves[0].start()
        moves[1].start()
        return moves

    tree = [climb(0, level0)]

    def place_of(n, sign):
        p = lax.rem(n + (CHUNKS // 2) * (sign < 0), CHUNKS)
        return lax.rem(2 * p, CHUNKS) + p // (CHUNKS // 2)

    def chunk(n, sign):
        b = lax.rem(second - sign * (n // CHUNKS) + RING, RING)
        q = lax.rem(first // PART + place_of(n, sign), CHUNKS)
        return pool.at[pl.ds((core * LINE + b * RING) * PER_CHIP + q * CHUNK, CHUNK)]

    def arrive(q):
        at = lax.rem(first // PART + q, CHUNKS)
        ref = pool.at[pl.ds(0, CHUNK if q else CHUNK - 2)]
        send(ref, ref, first_send, first_recv.at[at], sibling).wait_recv()

    def to_right(n):
        ref = chunk(n, 1)
        send(ref, ref, right_send, right_recv.at[n], right).start()

    def to_left(n):
        ref = chunk(n, -1)
        send(ref, ref, left_send, left_recv.at[n], left).start()

    def to_sibling(ref):
        send(ref, ref, sib_send, sib_recv, sibling).start()

    def spread_columns(t):
        turned = jnp.transpose(geo[HALO + t])
        for k in range(4):
            value = turned[:, k : k + 1]
            if k == 3:
                value = value * soften
            columns[t, k] = jnp.broadcast_to(value, (LEAF, 128))

    def add_tile(t, w, shift, before, slot):
        rows = geo[w]
        row_x, row_y, row_z, row_a = (rows[0:1] - shift, rows[1:2], rows[2:3], rows[3:4])
        for i in range(0, LEAF, 32):
            sides = []
            for lane in (0, 128):
                cut = slice(lane, lane + 128)
                dx = columns[t, 0, i : i + 32] - row_x[:, cut]
                dy = columns[t, 1, i : i + 32] - row_y[:, cut]
                dz = columns[t, 2, i : i + 32] - row_z[:, cut]
                total = dx * dx + soften + dy * dy + dz * dz
                guess = pl.reciprocal(total, approx=True)
                guess = guess * (2.0 - total * guess)
                sides.append((columns[t, 3, i : i + 32] * row_a[:, cut] * guess).astype(BF16))
            tile[slot, i : i + 32, :] = jnp.concatenate(sides, axis=1)
        near_terms[t] = before + lax.dot_general(window[w], tile[slot], NT, preferred_element_type=F32)

    def near_pair(p, slot):
        t, k = p // NNEAR, p % NNEAR
        w = (near_list_ref[k, t] - LEAVES * me + HALO) & (LEAVES + 2 * HALO - 1)
        add_tile(t, w, (t + HALO - w).astype(F32) * spacing, near_terms[t], slot)

    def encode(t, carry):
        for c in range(NFAR):
            entry = far_list_ref[t, c]
            layer, row, group = entry >> 9, (entry >> 6) & 7, (entry >> 2) & 1
            low, high = layer * RING + row, row * RING + layer + LINE
            place = low + group * (high - low)
            codes[t, c] = place * 8 + ((entry >> 5) & 1) * 4 + (entry & 3)
        return carry

    for t in range(LEAVES):
        spread_columns(t)

    def rejoin(height):
        tree[height][2].wait_recv()
        total = mine[height] + partner[height]
        tree.append(climb(height + 1, total[:, :RANK]))

    for n in range(CHUNKS // 2):
        arrive(2 * n)
        to_right(n)
        arrive(2 * n + 1)
        to_left(n)
    for n in range(CHUNKS // 2, CHUNKS):
        to_right(n)
        to_left(n)
    line = pool.at[pl.ds((core * LINE + second * RING) * PER_CHIP, RING * PER_CHIP)]
    to_sibling(line)
    rejoin(0)
    lax.fori_loop(0, LEAVES, encode, 0)
    for t in range(LEAVES):
        add_tile(t, HALO + t, 0.0, 0.0, t % TILES)
    for move in halos:
        move.wait_recv()

    def take(n, onward):
        ref = chunk(n + CHUNKS, 1)
        send(ref, ref, right_send, right_recv.at[n], right).wait_recv()
        if onward:
            send(ref, ref, right_send, right_recv.at[n + CHUNKS], right).start()
        ref_left = chunk(n + CHUNKS, -1)
        send(ref_left, ref_left, left_send, left_recv.at[n], left).wait_recv()
        if onward:
            send(ref_left, ref_left, left_send, left_recv.at[n + CHUNKS], left).start()
        to_sibling(ref)
        to_sibling(ref_left)

    def couple(height):
        tree[height][0].wait_recv()
        tree[height][1].wait_recv()
        cluster = me // 2**height
        low = jnp.where(cluster >= 2, below[height][:, :RANK], 0.0)
        high = jnp.where(cluster + 2 < devices // 2**height, above[height][:, :RANK], 0.0)
        return exact(low, upper_ref[height, 0]) + exact(high, upper_ref[height, 1])

    coupled = []
    def ring_step(n, carry):
        for k in range(SPLIT):
            take(SPLIT * n + k, True)
        for k in range(TILES):
            near_pair(TILES * n + k, k)
        return carry

    for place in range(5):
        for n in (2 * place, 2 * place + 1):
            ring_step(n, 0)
        if place in (0, 2):
            rejoin(1 + place // 2)
        if place in (1, 3):
            coupled.append(couple(place // 2))
    for p in range(TILES * 10, LEAVES * NNEAR):
        near_pair(p, p % TILES)
    coupled.append(couple(2))

    def last_step(n, carry):
        take(n, False)
        return carry

    for n in range(10 * SPLIT, 12 * SPLIT):
        last_step(n, 0)

    coupled.append(couple(UPLV))
    downward = coupled[UPLV]
    for height in range(UPLV - 1, -1, -1):
        downward = coupled[height] + exact(downward, up_ref[height, (me // 2**height) % 2], NT)
    pulled[...] = exact(downward, transfer[...], NT)

    for n in range(12 * SPLIT, STEPS):
        last_step(n, 0)

    coupling_load.wait()

    for move in halos + [m for moves in tree for m in moves]:
        move.wait_send()

    def sent(count, send_sem):
        ref = pool.at[pl.ds(0, count)]
        send(ref, ref, send_sem, sib_recv, sibling).wait_send()

    sent(2 * (2 * RING - 1), first_send)
    sent(STEPS * CHUNK, right_send)
    sent(STEPS * CHUNK, left_send)

    others = pool.at[pl.ds((1 - core) * LINE * PER_CHIP, LINE * PER_CHIP)]
    send(others, others, sib_send, sib_recv, sibling).wait_recv()

    for t in range(LEAVES):
        picked = []
        for c in range(0, NFAR, 2):
            two = []
            for k in range(2):
                code = codes[t, c + k]
                block = pool[code >> 1]
                turned = jnp.concatenate([block[:, RANK:], block[:, :RANK]], axis=1)
                two.append(jnp.where((code & 1) == k, block, turned))
            picked.append(two[0] * mask[0] + two[1] * mask[1])
        far = jnp.dot(jnp.concatenate(picked, axis=1), coupling[t], preferred_element_type=F32)
        leaf_far = (far + pulled[:, t * RANK : (t + 1) * RANK]).astype(BF16)
        back = jnp.dot(leaf_far, basis[t], preferred_element_type=F32)
        out_ref[:, t * LEAF : (t + 1) * LEAF] = (near_terms[t] + back).astype(BF16)

    sent(LINE * PER_CHIP, sib_send)


def solution(mesh):
    devices = mesh.shape["leaf"] * mesh.shape["sub"]

    def per_device(
        light,
        probes,
        near_list,
        far_list,
        leaf_basis,
        leaf_transfer,
        far_coupling,
        up_transfer,
        upper_coupling,
    ):
        any_space = pl.BlockSpec(memory_space=pl.ANY)
        vmem = pl.BlockSpec(memory_space=pltpu.VMEM)
        dma = pltpu.SemaphoreType.DMA
        slots = LEAVES + 2 * HALO
        return pl.pallas_call(
            functools.partial(kernel, devices),
            out_shape=pltpu.VMEM((LIGHTS, LEAVES * LEAF), BF16),
            in_specs=[any_space] * 9,
            out_specs=vmem,
            scratch_shapes=[
                pltpu.SMEM((NNEAR, LEAVES), jnp.int32),
                pltpu.SMEM((LEAVES, NFAR), jnp.int32),
                pltpu.VMEM((4, LEAVES * LEAF), BF16),
                pltpu.VMEM(up_transfer.shape, BF16),
                pltpu.VMEM(upper_coupling.shape, BF16),
                pltpu.VMEM((slots, LIGHTS, LEAF), BF16),
                pltpu.VMEM((slots, 8, LEAF), F32),
                pltpu.VMEM((LEAVES, 4, LEAF, 128), F32),
                pltpu.VMEM((LEAVES, RANK, LEAF), BF16),
                pltpu.VMEM((LEAVES * RANK, RANK), BF16),
                pltpu.VMEM((LEAVES, NFAR * RANK, RANK), BF16),
                pltpu.VMEM((2 * LINE * PER_CHIP, LIGHTS, 2 * RANK), BF16),
                pltpu.VMEM((2, LIGHTS, 2 * RANK), BF16),
                pltpu.VMEM((LEAVES, LIGHTS, LEAF), F32),
                pltpu.VMEM((LIGHTS, LEAVES * RANK), F32),
                pltpu.VMEM((TILES, LEAF, LEAF), BF16),
                pltpu.VMEM((UPLV + 1, LIGHTS, 2 * RANK), F32),
                pltpu.VMEM((UPLV, LIGHTS, 2 * RANK), F32),
                pltpu.VMEM((UPLV, LIGHTS, 2 * RANK), F32),
                pltpu.VMEM((UPLV + 1, LIGHTS, 2 * RANK), F32),
                pltpu.VMEM((UPLV + 1, LIGHTS, 2 * RANK), F32),
                pltpu.VMEM((2, LIGHTS, 2 * RANK), BF16),
                pltpu.SMEM((LEAVES, NFAR), jnp.int32),
                dma((8 + LEAVES,)),
                dma((4,)),
                dma((4,)),
                dma,
                dma((CHUNKS,)),
                dma,
                dma((STEPS,)),
                dma,
                dma((STEPS,)),
                dma,
                dma,
                dma((3 * (UPLV + 1),)),
                dma((3 * (UPLV + 1),)),
            ],
            compiler_params=pltpu.CompilerParams(
                collective_id=0, has_side_effects=True, vmem_limit_bytes=56 * 2**20
            ),
        )(
            light,
            probes,
            near_list.T,
            far_list,
            jnp.swapaxes(leaf_basis, 1, 2),
            leaf_transfer.reshape(LEAVES * RANK, RANK),
            far_coupling.reshape(LEAVES, NFAR * RANK, RANK),
            up_transfer,
            upper_coupling,
        )

    return jax.shard_map(
        per_device,
        mesh=mesh,
        in_specs=(
            P(None, ("leaf", "sub")),
            P(None, ("leaf", "sub")),
            P(("leaf", "sub"), None),
            P(("leaf", "sub"), None),
            P(("leaf", "sub"), None, None),
            P(("leaf", "sub"), None, None),
            P(("leaf", "sub"), None, None, None),
            P(),
            P(),
        ),
        out_specs=P(None, ("leaf", "sub")),
        check_vma=False,
    )
```
